32 devices in a mesh: dp: 8 (over y, x, core), tensor: 4 (over z).
Axes of the slice: x: 2, y: 2, z: 4, core: 2. Of those that a mesh axis runs over, the one named last changes fastest.
Arguments:
- layer_input: bfloat16 [16384, 1024], P(('dp', 'tensor')), may hold values from -6 to 6
- segments: int32 [16384], P('dp'), may hold values from 0 to 4, as said below
- norm_gain: float32 [1024], replicated, may hold values from 0.1 to 1.9
- w_query: bfloat16 [1024, 1024], P('dp', 'tensor'), may hold values from -0.1875 to 0.1875
- w_key: bfloat16 [1024, 1024], P('dp', 'tensor'), may hold values from -0.1875 to 0.1875
- w_value: bfloat16 [1024, 2048], P('dp', 'tensor'), may hold values from -0.1875 to 0.1875
- w_outgate: bfloat16 [1024, 2048], P('dp', 'tensor'), may hold values from -0.1875 to 0.1875
- w_beta: bfloat16 [1024, 8], P('dp', 'tensor'), may hold values from -0.1875 to 0.1875
- w_decay: bfloat16 [1024, 8], P('dp', 'tensor'), may hold values from -0.1875 to 0.1875
- conv_query: float32 [4, 1024], replicated, may hold values from -3 to 3
- conv_key: float32 [4, 1024], replicated, may hold values from -3 to 3
- conv_value: float32 [4, 2048], replicated, may hold values from -3 to 3
- decay_log: float32 [8], replicated, may hold values from -7 to 0
- decay_bias: float32 [8], replicated, may hold values from -3 to 3
- out_gain: float32 [256], replicated, may hold values from 0.1 to 1.9
- w_out: bfloat16 [2048, 1024], P('tensor', 'dp'), may hold values from -0.125 to 0.125
- ffn_gain: float32 [1024], replicated, may hold values from 0.1 to 1.9
- w_gate: bfloat16 [1024, 2816], P('dp', 'tensor'), may hold values from -0.1875 to 0.1875
- w_up: bfloat16 [1024, 2816], P('dp', 'tensor'), may hold values from -0.1875 to 0.1875
- w_down: bfloat16 [2816, 1024], P('tensor', 'dp'), may hold values from -0.109375 to 0.109375
- cotangent: bfloat16 [16384, 1024], P(('dp', 'tensor')), may hold values from -6 to 6
Outputs:
- layer_output: bfloat16 [16384, 1024], P(('dp', 'tensor'))
- grad_input: float32 [16384, 1024], P(('dp', 'tensor'))
- grad_norm_gain: float32 [1024], replicated
- grad_w_query: float32 [1024, 1024], P('dp', 'tensor')
- grad_w_key: float32 [1024, 1024], P('dp', 'tensor')
- grad_w_value: float32 [1024, 2048], P('dp', 'tensor')
- grad_w_outgate: float32 [1024, 2048], P('dp', 'tensor')
- grad_w_beta: float32 [1024, 8], P('dp', 'tensor')
- grad_w_decay: float32 [1024, 8], P('dp', 'tensor')
- grad_conv_query: float32 [4, 1024], replicated
- grad_conv_key: float32 [4, 1024], replicated
- grad_conv_value: float32 [4, 2048], replicated
- grad_decay_log: float32 [8], replicated
- grad_decay_bias: float32 [8], replicated
- grad_out_gain: float32 [256], replicated
- grad_w_out: float32 [2048, 1024], P('tensor', 'dp')
- grad_ffn_gain: float32 [1024], replicated
- grad_w_gate: float32 [1024, 2816], P('dp', 'tensor')
- grad_w_up: float32 [1024, 2816], P('dp', 'tensor')
- grad_w_down: float32 [2816, 1024], P('tensor', 'dp')
The draws below stay inside these ranges and needn't reach their ends.
Inputs may be any that keep to these rules, and one draw needn't show every extreme that they name: `segments`: within each group of 2048 consecutive tokens the segment numbers never fall; tokens with equal numbers form one packed sequence.
All inputs are finite; a program needn't handle non-finite values.
Results may differ from the reference program's by a relative error of at most 0.014.
The reference program's roundings to bfloat16 on the way count: a program that leaves them out, or rounds other values in their place, can miss the bound.
Values may be sent and summed in bfloat16 or wider, within the bound.
No kernel may reach another device: no remote copies, remote signals or barrier semaphores. Data moves between devices by JAX's collectives and lax.ppermute only.
A program may use at most 256 MiB of HBM per device.

```python
import jax
import jax.numpy as jnp
from jax import lax

D = 1024
H = 8
DK = 128
DV = 256
FF = 2816
KW = 4
SPAN = 128
TOK_DP = 2048
GROUPS = 8
TOKENS = 16384


def draw_segments(key, part):
    key = jax.random.fold_in(key, 11)
    subkeys = jax.random.split(key, 4)
    first_cut = jax.random.randint(subkeys[0], (GROUPS, 1), 1, TOK_DP // 8 + 1)
    early_cut = jax.random.randint(subkeys[1], (GROUPS, 1), 1, first_cut + 1)
    late_cut = jax.random.randint(subkeys[2], (GROUPS, 1), TOK_DP - TOK_DP // 8, TOK_DP)
    final_cut = jax.random.randint(subkeys[3], (GROUPS, 1), late_cut, TOK_DP)
    places = jnp.arange(TOK_DP, dtype=jnp.int32)[None, :]
    numbers = (places >= early_cut).astype(jnp.int32) + (places >= first_cut).astype(jnp.int32) + (places >= late_cut).astype(jnp.int32) + (places >= final_cut).astype(jnp.int32)
    return numbers.reshape(TOKENS)


def block_levels(key, extent, pieces, smallest, top_value):
    def one(dim, parts):
        draws = jax.random.uniform(jax.random.fold_in(jax.random.fold_in(key, 6), dim), (parts,), jnp.float32, smallest / len(pieces), top_value / len(pieces))
        return jnp.repeat(jnp.exp(draws), extent[dim] // parts).reshape((-1,) + (1,) * (len(extent) - dim - 1))

    level = one(*pieces[0])
    for cut in pieces[1:]:
        level = level * one(*cut)
    return level


def gaussian(stream_key, extent, scale, reach, shards=(), held_as=jnp.bfloat16):
    factor_of = block_levels(stream_key, extent, shards, -0.22, 0.18) if shards else 1.0
    entries = jax.random.normal(stream_key, extent, jnp.float32) * scale * factor_of
    return jnp.minimum(jnp.maximum(entries, -reach), reach).astype(held_as)


def setup_inputs(seed: int = 0) -> dict:
    streams_of = jax.random.split(jax.random.key(seed), 22)
    layer_input = gaussian(streams_of[0], (TOKENS, D), 1.0, 6.0, ((0, 32),))
    segments = draw_segments(jax.random.fold_in(streams_of[21], 71), 0)
    norm_gain = jnp.clip(1.0 + 0.18 * jax.random.normal(streams_of[2], (D,), jnp.float32), 0.1, 1.9)
    w_query = gaussian(streams_of[3], (D, H * DK), D ** -0.5, 0.1875, ((0, 8), (1, 4)))
    w_key = gaussian(streams_of[4], (D, H * DK), D ** -0.5, 0.1875, ((0, 8), (1, 4)))
    w_value = gaussian(streams_of[5], (D, H * DV), D ** -0.5, 0.1875, ((0, 8), (1, 4)))
    w_outgate = gaussian(streams_of[6], (D, H * DV), D ** -0.5, 0.1875, ((0, 8), (1, 4)))
    w_beta = gaussian(streams_of[7], (D, H), D ** -0.5, 0.1875, ((0, 8), (1, 4)))
    w_decay = gaussian(streams_of[8], (D, H), D ** -0.5, 0.1875, ((0, 8), (1, 4)))
    conv_query = gaussian(streams_of[9], (KW, H * DK), 0.5, 3.0, (), jnp.float32)
    conv_key = gaussian(streams_of[10], (KW, H * DK), 0.5, 3.0, (), jnp.float32)
    conv_value = gaussian(streams_of[11], (KW, H * DV), 0.5, 3.0, (), jnp.float32)
    decay_log = jnp.clip(jax.random.uniform(streams_of[12], (H,), jnp.float32, -7.0, 0.0), -7.0, 0.0)
    decay_bias = gaussian(streams_of[13], (H,), 1.0, 3.0, (), jnp.float32)
    out_gain = jnp.clip(1.0 + 0.18 * jax.random.normal(streams_of[14], (DV,), jnp.float32), 0.1, 1.9)
    w_out = gaussian(streams_of[15], (H * DV, D), (H * DV) ** -0.5, 0.125, ((0, 4), (1, 8)))
    ffn_gain = jnp.clip(1.0 + 0.18 * jax.random.normal(streams_of[16], (D,), jnp.float32), 0.1, 1.9)
    w_gate = gaussian(streams_of[17], (D, FF), D ** -0.5, 0.1875, ((0, 8), (1, 4)))
    w_up = gaussian(streams_of[18], (D, FF), D ** -0.5, 0.1875, ((0, 8), (1, 4)))
    w_down = gaussian(streams_of[19], (FF, D), FF ** -0.5, 0.109375, ((0, 4), (1, 8)))
    cotangent = gaussian(streams_of[20], (TOKENS, D), 1.0, 6.0, ((0, 32),))
    return {"layer_input": layer_input, "segments": segments, "norm_gain": norm_gain, "w_query": w_query, "w_key": w_key, "w_value": w_value, "w_outgate": w_outgate, "w_beta": w_beta, "w_decay": w_decay, "conv_query": conv_query, "conv_key": conv_key, "conv_value": conv_value, "decay_log": decay_log, "decay_bias": decay_bias, "out_gain": out_gain, "w_out": w_out, "ffn_gain": ffn_gain, "w_gate": w_gate, "w_up": w_up, "w_down": w_down, "cotangent": cotangent}


highest_precision = lax.Precision.HIGHEST

@jax.custom_vjp
def low(v):
    return lax.optimization_barrier(v.astype(jnp.bfloat16)).astype(jnp.float32)

@jax.custom_vjp
def low_back(v):
    return v

def low_keep(v):
    return (low(v), None)

def low_pass(kept, grad):
    return (grad,)

def back_keep(v):
    return (v, None)

def back_low(kept, grad):
    return (low(grad),)
low.defvjp(low_keep, low_pass)
low_back.defvjp(back_keep, back_low)

def exact_dot(left, right):
    return jnp.dot(left, right, precision=highest_precision, preferred_element_type=jnp.float32)

def rms_norm(values, gain):
    return values * lax.rsqrt(lax.optimization_barrier(jnp.mean(values * values, axis=-1, keepdims=True)) + 1e-06) * gain

def unit_rows(values):
    return values * lax.rsqrt(lax.optimization_barrier(jnp.sum(values * values, axis=-1, keepdims=True)) + 1e-06)

def shift_masks(segment_ids, width):
    masks_list = []
    for lag_count in range(1, width):
        earlier = jnp.concatenate([jnp.full((lag_count,), -1, jnp.int32), segment_ids[:-lag_count]])
        masks_list.append((segment_ids == earlier).astype(jnp.float32))
    return masks_list

def short_conv(values, weight, same_masks):
    total = values * weight[0]
    for lag_count in range(1, weight.shape[0]):
        shifted = jnp.pad(values, ((lag_count, 0), (0, 0)))[:values.shape[0]]
        total = total + shifted * same_masks[lag_count - 1][:, None] * weight[lag_count]
    return total

def mixer_inputs(proj_query, proj_key, proj_value, proj_beta, proj_decay, conv_query, conv_key, conv_value, decay_log, decay_bias, same_masks):
    length = proj_query.shape[0]
    heads_here = proj_beta.shape[1]
    query_rows = jax.nn.silu(short_conv(proj_query, conv_query, same_masks)).reshape(length, heads_here, -1)
    key_rows = jax.nn.silu(short_conv(proj_key, conv_key, same_masks)).reshape(length, heads_here, -1)
    value_rows = jax.nn.silu(short_conv(proj_value, conv_value, same_masks)).reshape(length, heads_here, -1)
    query_rows = unit_rows(query_rows) * query_rows.shape[-1] ** (-0.5)
    key_rows = unit_rows(key_rows)
    beta_rows = jax.nn.sigmoid(proj_beta)
    decay_rows = -jnp.exp(decay_log) * jax.nn.softplus(proj_decay + decay_bias)
    return (query_rows, key_rows, value_rows, beta_rows, decay_rows)

def gated_norm(outputs, proj_gate, gain):
    length, heads_here, width_value = outputs.shape
    normed = outputs * lax.rsqrt(lax.optimization_barrier(jnp.mean(outputs * outputs, axis=-1, keepdims=True)) + 1e-06) * gain
    return (normed * jax.nn.silu(proj_gate.reshape(length, heads_here, width_value))).reshape(length, -1)

def token_step(carried, sliced):
    query_now, key_now, value_now, beta_now, decay_now, keep_now = sliced
    carried = carried * (jnp.exp(decay_now) * keep_now)[:, None, None]
    predicted = jnp.einsum('hvd,hd->hv', carried, key_now, precision=highest_precision)
    update = beta_now[:, None] * (value_now - predicted)
    carried = carried + update[:, :, None] * key_now[:, None, :]
    return (carried, jnp.einsum('hvd,hd->hv', carried, query_now, precision=highest_precision))

def span_tokens(carried, sliced):
    return lax.scan(token_step, carried, sliced)

def token_delta(query_rows, key_rows, value_rows, beta_rows, decay_rows, keep_rows):
    length, heads_here, width_key = key_rows.shape
    width_value = value_rows.shape[-1]
    blocks = length // SPAN
    sliced = (query_rows.reshape(blocks, SPAN, heads_here, width_key), key_rows.reshape(blocks, SPAN, heads_here, width_key), value_rows.reshape(blocks, SPAN, heads_here, width_value), beta_rows.reshape(blocks, SPAN, heads_here), decay_rows.reshape(blocks, SPAN, heads_here), jnp.broadcast_to(keep_rows[:, None], (length, heads_here)).reshape(blocks, SPAN, heads_here))
    initial = jnp.zeros((heads_here, width_value, width_key), jnp.float32)
    last_state, outputs = lax.scan(jax.checkpoint(span_tokens), initial, sliced)
    return outputs.reshape(length, heads_here, width_value)

def group_layer(layer_rows, segment_ids, params):
    norm_gain, w_query, w_key, w_value, w_outgate, w_beta, w_decay, conv_query, conv_key, conv_value, decay_log, decay_bias, out_gain, w_out, ffn_gain, w_gate, w_up, w_down = params
    same_masks = shift_masks(segment_ids, conv_query.shape[0])
    normed = low(rms_norm(layer_rows, norm_gain))
    proj_query = low_back(exact_dot(normed, w_query))
    proj_key = low_back(exact_dot(normed, w_key))
    proj_value = low_back(exact_dot(normed, w_value))
    proj_gate = low_back(exact_dot(normed, w_outgate))
    proj_beta = low_back(exact_dot(normed, w_beta))
    proj_decay = low_back(exact_dot(normed, w_decay))
    query_rows, key_rows, value_rows, beta_rows, decay_rows = mixer_inputs(proj_query, proj_key, proj_value, proj_beta, proj_decay, conv_query, conv_key, conv_value, decay_log, decay_bias, same_masks)
    outputs = token_delta(query_rows, key_rows, value_rows, beta_rows, decay_rows, same_masks[0])
    gated = low(gated_norm(outputs, proj_gate, out_gain))
    attended = low_back(exact_dot(gated, w_out))
    middle = layer_rows + attended
    second = low(rms_norm(middle, ffn_gain))
    gate_rows = low_back(exact_dot(second, w_gate))
    up_rows = low_back(exact_dot(second, w_up))
    hidden = low(jax.nn.silu(gate_rows) * up_rows)
    return middle + low_back(exact_dot(hidden, w_down))

def reference(layer_input, segments, norm_gain, w_query, w_key, w_value, w_outgate, w_beta, w_decay, conv_query, conv_key, conv_value, decay_log, decay_bias, out_gain, w_out, ffn_gain, w_gate, w_up, w_down, cotangent):
    params = tuple((weight.astype(jnp.float32) for weight in (norm_gain, w_query, w_key, w_value, w_outgate, w_beta, w_decay, conv_query, conv_key, conv_value, decay_log, decay_bias, out_gain, w_out, ffn_gain, w_gate, w_up, w_down)))
    width_model = layer_input.shape[1]
    grouped = layer_input.astype(jnp.float32).reshape(-1, TOK_DP, width_model)
    segment_groups = segments.reshape(-1, TOK_DP)

    def whole_layer(grouped_rows, weights):
        block = jax.checkpoint(lambda paired: group_layer(paired[0], paired[1], weights))
        return lax.map(block, (grouped_rows, segment_groups))
    result, pullback = jax.vjp(whole_layer, grouped, params)
    grad_rows, grad_params = pullback(cotangent.astype(jnp.float32).reshape(grouped.shape))
    grad_norm_gain, grad_w_query, grad_w_key, grad_w_value, grad_w_outgate, grad_w_beta, grad_w_decay, grad_conv_query, grad_conv_key, grad_conv_value, grad_decay_log, grad_decay_bias, grad_out_gain, grad_w_out, grad_ffn_gain, grad_w_gate, grad_w_up, grad_w_down = grad_params
    return (result.reshape(layer_input.shape).astype(jnp.bfloat16), grad_rows.reshape(layer_input.shape), grad_norm_gain, grad_w_query, grad_w_key, grad_w_value, grad_w_outgate, grad_w_beta, grad_w_decay, grad_conv_query, grad_conv_key, grad_conv_value, grad_decay_log, grad_decay_bias, grad_out_gain, grad_w_out, grad_ffn_gain, grad_w_gate, grad_w_up, grad_w_down)
```

```python
from functools import partial

import jax
import jax.numpy as jnp
from jax import lax
from jax.experimental import pallas as pl
from jax.experimental.pallas import tpu as pltpu
from jax.sharding import PartitionSpec as P

CHUNK = 128
TINY = 1e-06
LANES = 128


def split_high(values):
    high = values.astype(jnp.bfloat16)
    return high, (values - high.astype(jnp.float32)).astype(jnp.bfloat16)


def contract(left, right, dims):
    return lax.dot_general(
        left, right, ((dims[:1], dims[1:]), ((), ())), preferred_element_type=jnp.float32
    )


def dot_one(left, right, dims=(1, 0)):
    return contract(left.astype(jnp.bfloat16), right.astype(jnp.bfloat16), dims)


def dot_three(left, right, dims=(1, 0)):
    left_high, left_low = split_high(left)
    right_high, right_low = split_high(right)
    return (
        contract(left_high, right_high, dims)
        + contract(left_high, right_low, dims)
        + contract(left_low, right_high, dims)
    )


def square_three(left, right):
    left_high, left_low = split_high(left)
    right_high, right_low = split_high(right)
    wide_left = jnp.concatenate([left_high, left_low], axis=1)
    row = jnp.concatenate([right_high, right_low], axis=1)
    product = contract(wide_left, jnp.concatenate([row, row], axis=0), (1, 0))
    width = right.shape[1]
    return product[:, :width] + product[:, width:]


def iota2(shape, axis):
    return lax.broadcasted_iota(jnp.int32, shape, axis)


def sigmoid(values):
    return 1.0 / (1.0 + jnp.exp(-values))


def softplus(values):
    return jnp.maximum(values, 0.0) + jnp.log1p(jnp.exp(-jnp.abs(values)))


def unit_inverses(lowers):
    rows = iota2((CHUNK, CHUNK), 0)
    cols = iota2((CHUNK, CHUNK), 1)
    differ = jnp.bitwise_xor(rows, cols)
    identity = jnp.where(rows == cols, 1.0, 0.0)
    block = 1
    results = None
    while block < CHUNK:
        pick = jnp.logical_and(differ >= block, differ < 2 * block)
        parts = [jnp.where(pick, lower, 0.0) for lower in lowers]
        if block == 1:
            results = [identity - part for part in parts]
        else:
            inner = [square_three(part, result) for part, result in zip(parts, results)]
            outer = [square_three(result, mid) for mid, result in zip(inner, results)]
            results = [result - out for result, out in zip(results, outer)]
        block *= 2
    return results


def head_scalars(small, head_ref):
    decay_scale = -jnp.exp(head_ref[0:1, :])
    shifted = small + head_ref[1:2, :]
    return sigmoid(small), decay_scale * softplus(shifted), decay_scale * sigmoid(shifted)


def running_sum(values, reverse=False):
    rows = iota2((CHUNK, CHUNK), 0)
    cols = iota2((CHUNK, CHUNK), 1)
    keep = (cols >= rows) if reverse else (rows >= cols)
    ones = jnp.where(keep, 1.0, 0.0).astype(jnp.bfloat16)
    high, low = split_high(values)
    lowest = (values - high.astype(jnp.float32) - low.astype(jnp.float32)).astype(jnp.bfloat16)
    return (
        contract(ones, high, (1, 0)) + contract(ones, low, (1, 0)) + contract(ones, lowest, (1, 0))
    )


def conv_rows(window_ref, aux, taps_ref, count, lo, hi):
    total = window_ref[8 : 8 + count, lo:hi] * taps_ref[0:1, lo:hi]
    for lag in range(1, taps_ref.shape[0]):
        shifted = window_ref[8 - lag : 8 - lag + count, lo:hi] * aux[:, lag - 1 : lag]
        total = total + shifted * taps_ref[lag : lag + 1, lo:hi]
    return total


def decay_parts(cumulative, cumulative_rows, aux, segment_row, lane):
    cum_col = cumulative[:, lane : lane + 1]
    cum_row = cumulative_rows[lane : lane + 1, :]
    rows = iota2((CHUNK, CHUNK), 0)
    cols = iota2((CHUNK, CHUNK), 1)
    keep = jnp.logical_and(rows >= cols, aux[:, 5:6] == segment_row)
    matrix = jnp.where(keep, jnp.exp(jnp.minimum(cum_col - cum_row, 0.0)), 0.0)
    last = cum_col[CHUNK - 1 : CHUNK, :]
    growth = jnp.exp(cum_col) * aux[:, 3:4]
    tail = jnp.exp(last - cum_col) * aux[:, 4:5]
    carry = jnp.exp(last) * aux[CHUNK - 1 : CHUNK, 3:4]
    return matrix, growth, tail, carry


def forward_body(
    sizes,
    rank_ref,
    proj_ref,
    aux_ref,
    segment_ref,
    taps_ref,
    head_ref,
    gain_ref,
    gated_ref,
    out_ref,
    fresh_ref,
    state_ref,
    inverse_ref,
    window_ref,
    carried_ref,
):
    heads, dk, dv, chunks = sizes
    count = chunks * CHUNK
    keys, conv_cols = heads * dk, heads * (2 * dk + dv)
    gate_at, small_at = conv_cols, conv_cols + heads * dv

    @pl.when(pl.program_id(0) == 0)
    def start():
        window_ref[0:8, :] = jnp.zeros((8, conv_cols), jnp.float32)
        carried_ref[...] = jnp.zeros(carried_ref.shape, jnp.float32)

    aux = aux_ref[...]
    window_ref[8 : 8 + count, :] = proj_ref[:, :conv_cols]
    beta_all, decay_all, _ = head_scalars(proj_ref[:, small_at : small_at + LANES], head_ref)

    queries, key_rows, values = [], [], []
    for head in range(heads):
        mixed = conv_rows(window_ref, aux, taps_ref, count, head * dk, (head + 1) * dk)
        mixed = mixed * sigmoid(mixed)
        queries.append(
            mixed * (lax.rsqrt(jnp.sum(mixed * mixed, axis=1, keepdims=True) + TINY) * dk**-0.5)
        )
        mixed = conv_rows(window_ref, aux, taps_ref, count, keys + head * dk, keys + (head + 1) * dk)
        mixed = mixed * sigmoid(mixed)
        key_rows.append(mixed * lax.rsqrt(jnp.sum(mixed * mixed, axis=1, keepdims=True) + TINY))
        at = 2 * keys + head * dv
        mixed = conv_rows(window_ref, aux, taps_ref, count, at, at + dv)
        values.append(mixed * sigmoid(mixed))

    strict = iota2((CHUNK, CHUNK), 0) > iota2((CHUNK, CHUNK), 1)
    items = []
    lowers = []
    for chunk in range(chunks):
        span = slice(chunk * CHUNK, (chunk + 1) * CHUNK)
        cumulative = running_sum(decay_all[span])
        cumulative_rows = jnp.transpose(cumulative)
        for head in range(heads):
            matrix, growth, tail, carry = decay_parts(
                cumulative, cumulative_rows, aux[span], segment_ref[chunk], heads + head
            )
            beta = beta_all[span, head : head + 1]
            query, key = queries[head][span], key_rows[head][span]
            lowers.append(
                jnp.where(strict, beta * matrix * dot_three(key, key, (1, 1)), 0.0)
            )
            scores = dot_three(query, key, (1, 1)) * matrix
            items.append((span, chunk, head, beta, query, key, scores, growth, tail, carry))
    inverses = unit_inverses(lowers)
    for (span, chunk, head, beta, query, key, scores, growth, tail, carry), inverse in zip(
        items, inverses
    ):
        wide = slice(head * dv, (head + 1) * dv)
        inverse_ref[span, head * CHUNK : (head + 1) * CHUNK] = inverse
        state = carried_ref[head]
        state_ref[chunk, :, wide] = state
        right = beta * (values[head][span] - growth * dot_three(key, state))
        fresh = dot_three(inverse, right)
        fresh_ref[span, wide] = fresh
        carried_ref[head] = carry * state + dot_three(tail * key, fresh, (0, 0))
        emitted = growth * dot_three(query, state) + dot_three(scores, fresh)
        out_ref[span, wide] = emitted
        gate = proj_ref[span, gate_at + head * dv : gate_at + (head + 1) * dv]
        scale = lax.rsqrt(jnp.mean(emitted * emitted, axis=1, keepdims=True) + TINY)
        gated_ref[span, wide] = (
            emitted * scale * gain_ref[...] * (gate * sigmoid(gate))
        ).astype(jnp.bfloat16)
    window_ref[0:8, :] = proj_ref[count - 8 : count, :conv_cols]


def backward_body(
    sizes,
    rank_ref,
    proj_ref,
    before_ref,
    aux_ref,
    segment_ref,
    taps_ref,
    head_ref,
    gain_ref,
    out_ref,
    fresh_ref,
    state_ref,
    inverse_ref,
    grad_ref,
    dproj_ref,
    dtaps_ref,
    dgain_ref,
    dhead_ref,
    window_ref,
    later_ref,
    carried_ref,
):
    heads, dk, dv, chunks = sizes
    count = chunks * CHUNK
    keys, conv_cols = heads * dk, heads * (2 * dk + dv)
    gate_at, small_at = conv_cols, conv_cols + heads * dv
    lags = taps_ref.shape[0]

    @pl.when(pl.program_id(0) == 0)
    def start():
        later_ref[count : count + 8, :] = jnp.zeros((8, conv_cols), jnp.float32)
        carried_ref[...] = jnp.zeros(carried_ref.shape, jnp.float32)
        dtaps_ref[...] = jnp.zeros(dtaps_ref.shape, jnp.float32)
        dgain_ref[...] = jnp.zeros(dgain_ref.shape, jnp.float32)
        dhead_ref[...] = jnp.zeros(dhead_ref.shape, jnp.float32)

    aux = aux_ref[...]
    first = pl.program_id(0) == pl.num_programs(0) - 1
    window_ref[0:8, :] = jnp.where(first, 0.0, before_ref[:, :conv_cols])
    window_ref[8 : 8 + count, :] = proj_ref[:, :conv_cols]
    beta_all, decay_all, slope_all = head_scalars(
        proj_ref[:, small_at : small_at + LANES], head_ref
    )
    lane = iota2((CHUNK, LANES), 1)
    row_at = iota2((LANES, CHUNK), 0)
    strict = iota2((CHUNK, CHUNK), 0) > iota2((CHUNK, CHUNK), 1)

    def activated(lo, width):
        mixed = conv_rows(window_ref, aux, taps_ref, count, lo, lo + width)
        gate = sigmoid(mixed)
        return mixed * gate, gate * (1.0 + mixed * (1.0 - gate))

    for head in range(heads):
        wide = slice(head * dv, (head + 1) * dv)
        emitted = out_ref[:, wide]
        scale = lax.rsqrt(jnp.mean(emitted * emitted, axis=1, keepdims=True) + TINY)
        normed = emitted * scale
        at = gate_at + head * dv
        gate = proj_ref[:, at : at + dv]
        sig = sigmoid(gate)
        upper = grad_ref[:, wide].astype(jnp.float32)
        with_gate = upper * (gate * sig)
        dgain_ref[...] += jnp.sum((with_gate * normed).reshape(count // 8, 8, dv), axis=0)
        dproj_ref[:, at : at + dv] = (
            upper * normed * gain_ref[...] * (sig * (1.0 + gate * (1.0 - sig)))
        ).astype(jnp.bfloat16)
        dnormed = with_gate * gain_ref[...]
        dout_all = scale * (
            dnormed - normed * jnp.mean(dnormed * normed, axis=1, keepdims=True)
        )

        query_raw, query_slope = activated(head * dk, dk)
        query_scale = lax.rsqrt(jnp.sum(query_raw * query_raw, axis=1, keepdims=True) + TINY)
        query_unit = query_raw * query_scale
        key_raw, key_slope = activated(keys + head * dk, dk)
        key_scale = lax.rsqrt(jnp.sum(key_raw * key_raw, axis=1, keepdims=True) + TINY)
        key_all = key_raw * key_scale
        value_all, value_slope = activated(2 * keys + head * dv, dv)
        query_all = query_unit * dk**-0.5

        for chunk in reversed(range(chunks)):
            span = slice(chunk * CHUNK, (chunk + 1) * CHUNK)
            cumulative = running_sum(decay_all[span])
            matrix, growth, tail, carry = decay_parts(
                cumulative, jnp.transpose(cumulative), aux[span], segment_ref[chunk], heads + head
            )
            beta = beta_all[span, head : head + 1]
            query, key, value = query_all[span], key_all[span], value_all[span]
            inverse = inverse_ref[span, head * CHUNK : (head + 1) * CHUNK]
            state = state_ref[chunk, :, wide]
            fresh = fresh_ref[span, wide]
            dout = dout_all[span]
            key_products = dot_three(key, key, (1, 1)) * matrix
            scores = dot_three(query, key, (1, 1)) * matrix

            dstate = carried_ref[head]
            dfresh = dot_three(scores, dout, (0, 0)) + dot_three(tail * key, dstate)
            dright = dot_three(inverse, dfresh, (0, 0))
            carried_ref[head] = (
                carry * dstate
                + dot_three(growth * query, dout, (0, 0))
                - dot_three((growth * beta) * key, dright, (0, 0))
            )
            dscores = dot_three(dout, fresh, (1, 1))
            dlower = jnp.where(strict, -dot_three(dright, fresh, (1, 1)), 0.0)
            out_state = dot_three(dout, state, (1, 1))
            right_state = dot_three(dright, state, (1, 1))
            fresh_state = dot_three(fresh, dstate, (1, 1))
            dscores_key = dscores * matrix
            dlower_key = dlower * matrix * beta
            dquery = growth * out_state + dot_three(dscores_key, key)
            dkey = (
                tail * fresh_state
                + dot_three(dscores_key, query, (0, 0))
                - (growth * beta) * right_state
                + dot_three(dlower_key, key)
                + dot_three(dlower_key, key, (0, 0))
            )
            dvalue = beta * dright
            right_key = jnp.sum(right_state * key, axis=1, keepdims=True)
            dbeta = (
                jnp.sum(dright * value, axis=1, keepdims=True)
                - growth * right_key
                + jnp.sum(dlower * key_products, axis=1, keepdims=True)
            )
            dgrowth = jnp.sum(out_state * query, axis=1, keepdims=True) - beta * right_key
            dtail = jnp.sum(fresh_state * key, axis=1, keepdims=True)
            dcarry = jnp.sum(jnp.sum(dstate * state, axis=1, keepdims=True), axis=0, keepdims=True)
            dgap = dscores * scores + dlower * beta * key_products
            tail_term = dtail * tail
            last_term = jnp.sum(tail_term, axis=0, keepdims=True) + dcarry * carry
            is_last = iota2((CHUNK, 1), 0) == CHUNK - 1
            dcum = (
                jnp.sum(dgap, axis=1, keepdims=True)
                + dgrowth * growth
                - tail_term
                + jnp.where(is_last, last_term, 0.0)
            )
            down = jnp.sum(dgap, axis=0, keepdims=True)
            columns = jnp.transpose(jnp.where(row_at == heads + head, down, 0.0))
            ddecay = running_sum(jnp.where(lane == heads + head, dcum, 0.0) - columns, True)
            dbeta_lane = jnp.where(lane == head, dbeta, 0.0)
            dshift = ddecay * slope_all[span]
            dhead_ref[0:8, :] += jnp.sum(
                (ddecay * decay_all[span]).reshape(CHUNK // 8, 8, LANES), axis=0
            )
            dhead_ref[8:16, :] += jnp.sum(dshift.reshape(CHUNK // 8, 8, LANES), axis=0)
            sig_beta = beta_all[span]
            dsmall = dbeta_lane * (sig_beta * (1.0 - sig_beta)) + dshift
            if head == 0:
                small_parts = {} if chunk == chunks - 1 else small_parts
                small_parts[chunk] = dsmall
            else:
                small_parts[chunk] = small_parts[chunk] + dsmall

            def unit_back(grad, unit, scale_col):
                return scale_col * (grad - unit * jnp.sum(grad * unit, axis=1, keepdims=True))

            rows_at = slice(chunk * CHUNK, (chunk + 1) * CHUNK)
            later_ref[rows_at, head * dk : (head + 1) * dk] = (
                unit_back(dquery * dk**-0.5, query_unit[span], query_scale[span])
                * query_slope[span]
            )
            later_ref[rows_at, keys + head * dk : keys + (head + 1) * dk] = (
                unit_back(dkey, key, key_scale[span]) * key_slope[span]
            )
            at = 2 * keys + head * dv
            later_ref[rows_at, at : at + dv] = dvalue * value_slope[span]

    for chunk in range(chunks):
        span = slice(chunk * CHUNK, (chunk + 1) * CHUNK)
        dproj_ref[span, small_at : small_at + LANES] = small_parts[chunk].astype(jnp.bfloat16)

    block = 256
    for lo in range(0, conv_cols, block):
        hi = lo + block
        here = later_ref[0:count, lo:hi]
        total = here * taps_ref[0:1, lo:hi]
        dtaps_ref[0:8, lo:hi] += jnp.sum(
            (here * window_ref[8 : 8 + count, lo:hi]).reshape(count // 8, 8, block), axis=0
        )
        for lag in range(1, lags):
            ahead = later_ref[lag : lag + count, lo:hi] * aux[:, 5 + lag : 6 + lag]
            total = total + ahead * taps_ref[lag : lag + 1, lo:hi]
            shifted = window_ref[8 - lag : 8 - lag + count, lo:hi] * aux[:, lag - 1 : lag]
            dtaps_ref[8 * lag : 8 * lag + 8, lo:hi] += jnp.sum(
                (here * shifted).reshape(count // 8, 8, block), axis=0
            )
        dproj_ref[:, lo:hi] = total.astype(jnp.bfloat16)
    later_ref[count : count + 8, :] = later_ref[0:8, :]


FORWARD_CHUNKS = 2
BACKWARD_CHUNKS = 1


def whole_block(array):
    return pl.BlockSpec(array.shape, lambda step, rank: (0,) * array.ndim)


def mixer_forward(rank, proj, aux, segment_rows, taps, head_rows, gain, heads, dk, dv):
    length, width = proj.shape
    chunks = FORWARD_CHUNKS
    count = chunks * CHUNK
    steps = length // count
    conv_cols = heads * (2 * dk + dv)
    rows = lambda cols: pl.BlockSpec((count, cols), lambda step, rank: (step, 0))
    return pl.pallas_call(
        partial(forward_body, (heads, dk, dv, chunks)),
        grid_spec=pltpu.PrefetchScalarGridSpec(
            num_scalar_prefetch=1,
            grid=(steps,),
            in_specs=[
                rows(width),
                rows(LANES),
                pl.BlockSpec((chunks, 1, CHUNK), lambda step, rank: (step, 0, 0)),
                whole_block(taps),
                whole_block(head_rows),
                whole_block(gain),
            ],
            out_specs=[
                rows(heads * dv),
                rows(heads * dv),
                rows(heads * dv),
                pl.BlockSpec((chunks, dk, heads * dv), lambda step, rank: (step, 0, 0)),
                rows(heads * CHUNK),
            ],
            scratch_shapes=[
                pltpu.VMEM((8 + count, conv_cols), jnp.float32),
                pltpu.VMEM((heads, dk, dv), jnp.float32),
            ],
        ),
        out_shape=[
            jax.ShapeDtypeStruct((length, heads * dv), jnp.bfloat16),
            jax.ShapeDtypeStruct((length, heads * dv), jnp.float32),
            jax.ShapeDtypeStruct((length, heads * dv), jnp.float32),
            jax.ShapeDtypeStruct((length // CHUNK, dk, heads * dv), jnp.float32),
            jax.ShapeDtypeStruct((length, heads * CHUNK), jnp.float32),
        ],
        compiler_params=pltpu.CompilerParams(vmem_limit_bytes=48 * 2**20),
        cost_estimate=pl.CostEstimate(
            flops=80 * 10**9, bytes_accessed=length * width * 12, transcendentals=0
        ),
        name="mixer_forward",
    )(rank, proj, aux, segment_rows, taps, head_rows, gain)


def mixer_backward(
    rank, proj, aux, segment_rows, taps, head_rows, gain, saved, grad, heads, dk, dv
):
    length, width = proj.shape
    chunks = BACKWARD_CHUNKS
    count = chunks * CHUNK
    steps = length // count
    conv_cols = heads * (2 * dk + dv)
    out, fresh, states, inverses = saved
    place = lambda step: steps - 1 - step
    rows = lambda cols: pl.BlockSpec((count, cols), lambda step, rank: (place(step), 0))
    lags = taps.shape[0]
    before = pl.BlockSpec(
        (8, width), lambda step, rank: (jnp.maximum(place(step) * (count // 8) - 1, 0), 0)
    )
    whole = lambda shape: pl.BlockSpec(shape, lambda step, rank: (0, 0))
    return pl.pallas_call(
        partial(backward_body, (heads, dk, dv, chunks)),
        grid_spec=pltpu.PrefetchScalarGridSpec(
            num_scalar_prefetch=1,
            grid=(steps,),
            in_specs=[
                rows(width),
                before,
                rows(LANES),
                pl.BlockSpec((chunks, 1, CHUNK), lambda step, rank: (place(step), 0, 0)),
                whole_block(taps),
                whole_block(head_rows),
                whole_block(gain),
                rows(heads * dv),
                rows(heads * dv),
                pl.BlockSpec((chunks, dk, heads * dv), lambda step, rank: (place(step), 0, 0)),
                rows(heads * CHUNK),
                rows(heads * dv),
            ],
            out_specs=[
                rows(width),
                whole((8 * lags, conv_cols)),
                whole((8, dv)),
                whole((16, LANES)),
            ],
            scratch_shapes=[
                pltpu.VMEM((8 + count, conv_cols), jnp.float32),
                pltpu.VMEM((8 + count, conv_cols), jnp.float32),
                pltpu.VMEM((heads, dk, dv), jnp.float32),
            ],
        ),
        out_shape=[
            jax.ShapeDtypeStruct((length, width), jnp.bfloat16),
            jax.ShapeDtypeStruct((8 * lags, conv_cols), jnp.float32),
            jax.ShapeDtypeStruct((8, dv), jnp.float32),
            jax.ShapeDtypeStruct((16, LANES), jnp.float32),
        ],
        compiler_params=pltpu.CompilerParams(vmem_limit_bytes=48 * 2**20),
        cost_estimate=pl.CostEstimate(
            flops=160 * 10**9, bytes_accessed=length * width * 16, transcendentals=0
        ),
        name="mixer_backward",
    )(
        rank, proj, proj, aux, segment_rows, taps, head_rows, gain,
        out, fresh, states, inverses, grad,
    )


def segment_columns(segments):
    length = segments.shape[0]
    blocks = segments.reshape(-1, CHUNK)

    def earlier(lag):
        return jnp.concatenate([jnp.full((lag,), -1, jnp.int32), segments[:-lag]])

    def later(lag):
        return jnp.concatenate([segments[lag:], jnp.full((lag,), -1, jnp.int32)])

    same = [segments == earlier(lag) for lag in (1, 2, 3)]
    before = earlier(1).reshape(-1, CHUNK)[:, :1]
    same.append((blocks == before).reshape(length))
    same.append((blocks == blocks[:, -1:]).reshape(length))
    columns = [one.astype(jnp.float32) for one in same] + [segments.astype(jnp.float32)]
    columns += [(segments == later(lag)).astype(jnp.float32) for lag in (1, 2, 3)]
    table = jnp.stack(columns, axis=1)
    return jnp.pad(table, ((0, 0), (0, LANES - len(columns))))


def rms_parts(values):
    return lax.rsqrt(jnp.mean(values * values, axis=-1, keepdims=True) + TINY)


def rms_back(grad, gain, normed, scale):
    scaled = grad * gain
    return scale * (scaled - normed * jnp.mean(scaled * normed, axis=-1, keepdims=True))


def padded(array, width):
    return jnp.pad(array, ((0, 0), (0, width - array.shape[1])))


def product(left, right, left_dim, right_dim):
    return lax.dot_general(
        left, right, (((left_dim,), (right_dim,)), ((), ())), preferred_element_type=jnp.float32
    )


def up_to(size, unit):
    return -(-size // unit) * unit


def shards(
    layer_input,
    segments,
    norm_gain,
    w_query,
    w_key,
    w_value,
    w_outgate,
    w_beta,
    w_decay,
    conv_query,
    conv_key,
    conv_value,
    decay_log,
    decay_bias,
    out_gain,
    w_out,
    ffn_gain,
    w_gate,
    w_up,
    w_down,
    cotangent,
):
    tensor_rank = lax.axis_index("tensor")
    ranks = lax.axis_size("tensor")
    key_cols, value_cols, heads = w_query.shape[1], w_value.shape[1], w_beta.shape[1]
    dk, dv = key_cols // heads, value_cols // heads
    units = w_gate.shape[1]
    unit_cols = up_to(units, 256)
    conv_cols = 2 * key_cols + value_cols
    gate_at, small_at = conv_cols, conv_cols + value_cols

    joined = lax.all_gather(
        padded(
            jnp.concatenate([w_query, w_key, w_value, w_outgate, w_beta, w_decay], axis=1),
            small_at + LANES,
        ),
        "dp",
        axis=0,
        tiled=True,
    )
    rest = lax.all_gather(
        jnp.concatenate(
            [w_out.T, padded(w_gate, unit_cols), padded(w_up, unit_cols), padded(w_down.T, unit_cols)],
            axis=1,
        ),
        "dp",
        axis=0,
        tiled=True,
    )
    cut_out, cut_down = value_cols, value_cols + 2 * unit_cols
    out_full, pair_full, down_full = (
        rest[:, :cut_out],
        rest[:, cut_out:cut_down],
        rest[:, cut_down:],
    )

    residual = layer_input.astype(jnp.float32)
    first_scale = rms_parts(residual)
    first_normed = residual * first_scale
    mixer_rows = lax.all_gather(
        (first_normed * norm_gain).astype(jnp.bfloat16), "tensor", axis=0, tiled=True
    )
    projected = product(mixer_rows, joined, 1, 0)

    def local(array, width):
        return lax.dynamic_slice_in_dim(array, tensor_rank * width, width, array.ndim - 1)

    taps = jnp.concatenate(
        [local(conv_query, key_cols), local(conv_key, key_cols), local(conv_value, value_cols)],
        axis=1,
    )
    head_rows = jnp.pad(
        jnp.stack([local(decay_log, heads), local(decay_bias, heads)]),
        ((0, 6), (heads, LANES - 2 * heads)),
    )
    gain_row = out_gain[None, :]
    aux = segment_columns(segments)
    segment_rows = segments.astype(jnp.float32).reshape(-1, 1, CHUNK)
    rank = tensor_rank.astype(jnp.int32).reshape(1)
    gated, *saved = mixer_forward(
        rank, projected, aux, segment_rows, taps, head_rows, gain_row, heads, dk, dv
    )
    attended = lax.psum_scatter(
        product(gated, out_full, 1, 1).astype(jnp.bfloat16),
        "tensor",
        scatter_dimension=0,
        tiled=True,
    ).astype(jnp.float32)
    middle = residual + attended
    second_scale = rms_parts(middle)
    second_normed = middle * second_scale
    ffn_rows = lax.all_gather(
        (second_normed * ffn_gain).astype(jnp.bfloat16), "tensor", axis=0, tiled=True
    )
    cot_rows = lax.all_gather(cotangent, "tensor", axis=0, tiled=True)
    pair = product(ffn_rows, pair_full, 1, 0)
    gate_rows, up_rows = pair[:, :unit_cols], pair[:, unit_cols:]
    sig = jax.nn.sigmoid(gate_rows)
    hidden = (gate_rows * sig * up_rows).astype(jnp.bfloat16)
    grad_hidden = product(cot_rows, down_full, 1, 0)
    grad_pair = jnp.concatenate(
        [
            (grad_hidden * up_rows * sig * (1.0 + gate_rows * (1.0 - sig))).astype(jnp.bfloat16),
            (grad_hidden * gate_rows * sig).astype(jnp.bfloat16),
        ],
        axis=1,
    )
    grad_second = lax.psum_scatter(
        product(grad_pair, pair_full, 1, 1).astype(jnp.bfloat16),
        "tensor",
        scatter_dimension=0,
        tiled=True,
    ).astype(jnp.float32)
    grad_middle = cotangent.astype(jnp.float32) + rms_back(
        grad_second, ffn_gain, second_normed, second_scale
    )
    attn_rows = lax.all_gather(
        grad_middle.astype(jnp.bfloat16), "tensor", axis=0, tiled=True
    )
    ffn_out = lax.psum_scatter(
        product(hidden, down_full, 1, 1).astype(jnp.bfloat16),
        "tensor",
        scatter_dimension=0,
        tiled=True,
    ).astype(jnp.float32)
    layer_output = (middle + ffn_out).astype(jnp.bfloat16)
    grad_gated = product(attn_rows, out_full, 1, 0)
    grad_proj, dtaps, dgain, dhead = mixer_backward(
        rank, projected, aux, segment_rows, taps, head_rows, gain_row, saved, grad_gated, heads, dk, dv
    )
    grad_rest = jnp.concatenate(
        [
            product(attn_rows, gated, 0, 0),
            product(ffn_rows, grad_pair, 0, 0),
            product(cot_rows, hidden, 0, 0),
        ],
        axis=1,
    )
    grad_joined = product(mixer_rows, grad_proj, 0, 0)
    grad_first = lax.psum_scatter(
        product(grad_proj, joined, 1, 1).astype(jnp.bfloat16),
        "tensor",
        scatter_dimension=0,
        tiled=True,
    ).astype(jnp.float32)
    grad_input = grad_middle + rms_back(grad_first, norm_gain, first_normed, first_scale)

    grad_norm_gain = jnp.sum(joined.astype(jnp.float32) * grad_joined, axis=1) / norm_gain
    grad_ffn_gain = (
        jnp.sum(
            pair_full.astype(jnp.float32) * grad_rest[:, cut_out:cut_down], axis=1
        )
        / ffn_gain
    )
    summed_rest = lax.psum_scatter(
        grad_rest.astype(jnp.bfloat16), "dp", scatter_dimension=0, tiled=True
    ).astype(jnp.float32)
    summed_joined = lax.psum_scatter(
        grad_joined.astype(jnp.bfloat16), "dp", scatter_dimension=0, tiled=True
    ).astype(jnp.float32)

    lags = taps.shape[0]
    mine = jnp.concatenate(
        [
            jnp.sum(dtaps.reshape(lags, 8, conv_cols), axis=1).reshape(-1),
            jnp.sum(dhead[0:8], axis=0)[heads : 2 * heads],
            jnp.sum(dhead[8:16], axis=0)[heads : 2 * heads],
        ]
    )
    placed = jnp.where((jnp.arange(ranks) == tensor_rank)[:, None], mine[None, :], 0.0)
    vector = jnp.concatenate(
        [grad_norm_gain, grad_ffn_gain, jnp.sum(dgain, axis=0), placed.reshape(-1)]
    )
    small = lax.psum(vector, ("dp", "tensor"))
    width = norm_gain.shape[0]
    sections = small[2 * width + dv :].reshape(ranks, -1)
    taps_all = sections[:, : lags * conv_cols].reshape(ranks, lags, conv_cols).transpose(1, 0, 2)
    logs_all = sections[:, lags * conv_cols :]

    def columns(lo, hi):
        return summed_joined[:, lo:hi]

    return (
        layer_output,
        grad_input,
        small[:width],
        columns(0, key_cols),
        columns(key_cols, 2 * key_cols),
        columns(2 * key_cols, conv_cols),
        columns(gate_at, small_at),
        columns(small_at, small_at + heads),
        columns(small_at + heads, small_at + 2 * heads),
        taps_all[:, :, :key_cols].reshape(lags, -1),
        taps_all[:, :, key_cols : 2 * key_cols].reshape(lags, -1),
        taps_all[:, :, 2 * key_cols :].reshape(lags, -1),
        logs_all[:, :heads].reshape(-1),
        logs_all[:, heads:].reshape(-1),
        small[2 * width : 2 * width + dv],
        summed_rest[:, :cut_out].T,
        small[width : 2 * width],
        summed_rest[:, cut_out : cut_out + units],
        summed_rest[:, cut_out + unit_cols : cut_out + unit_cols + units],
        summed_rest[:, cut_down : cut_down + units].T,
    )


def solution(mesh):
    in_specs = (
        P(("dp", "tensor"), None),
        P("dp"),
        P(),
        P("dp", "tensor"),
        P("dp", "tensor"),
        P("dp", "tensor"),
        P("dp", "tensor"),
        P("dp", "tensor"),
        P("dp", "tensor"),
        P(),
        P(),
        P(),
        P(),
        P(),
        P(),
        P("tensor", "dp"),
        P(),
        P("dp", "tensor"),
        P("dp", "tensor"),
        P("tensor", "dp"),
        P(("dp", "tensor"), None),
    )
    out_specs = (
        P(("dp", "tensor"), None),
        P(("dp", "tensor"), None),
        P(),
        P("dp", "tensor"),
        P("dp", "tensor"),
        P("dp", "tensor"),
        P("dp", "tensor"),
        P("dp", "tensor"),
        P("dp", "tensor"),
        P(),
        P(),
        P(),
        P(),
        P(),
        P(),
        P("tensor", "dp"),
        P(),
        P("dp", "tensor"),
        P("dp", "tensor"),
        P("tensor", "dp"),
    )
    return jax.shard_map(shards, mesh=mesh, in_specs=in_specs, out_specs=out_specs, check_vma=False)
```

```python
from functools import partial

import jax
import jax.numpy as jnp
from jax import lax
from jax.experimental import pallas as pl
from jax.experimental.layout import Layout, with_layout_constraint
from jax.experimental.pallas import tpu as pltpu
from jax.sharding import PartitionSpec as P

CHUNK = 128
TINY = 1e-06
LANES = 128


def split_high(values):
    high = values.astype(jnp.bfloat16)
    return high, (values - high.astype(jnp.float32)).astype(jnp.bfloat16)


def contract(left, right, dims):
    return lax.dot_general(
        left, right, ((dims[:1], dims[1:]), ((), ())), preferred_element_type=jnp.float32
    )


def dot_one(left, right, dims=(1, 0)):
    return contract(left.astype(jnp.bfloat16), right.astype(jnp.bfloat16), dims)


def dot_three(left, right, dims=(1, 0)):
    left_high, left_low = split_high(left)
    right_high, right_low = split_high(right)
    return (
        contract(left_high, right_high, dims)
        + contract(left_high, right_low, dims)
        + contract(left_low, right_high, dims)
    )


def square_three(left, right):
    left_high, left_low = split_high(left)
    right_high, right_low = split_high(right)
    wide_left = jnp.concatenate([left_high, left_low], axis=1)
    row = jnp.concatenate([right_high, right_low], axis=1)
    product = contract(wide_left, jnp.concatenate([row, row], axis=0), (1, 0))
    width = right.shape[1]
    return product[:, :width] + product[:, width:]


def iota2(shape, axis):
    return lax.broadcasted_iota(jnp.int32, shape, axis)


def sigmoid(values):
    return 1.0 / (1.0 + jnp.exp(-values))


def softplus(values):
    return jnp.maximum(values, 0.0) + jnp.log1p(jnp.exp(-jnp.abs(values)))


def unit_inverses(lowers):
    rows = iota2((CHUNK, CHUNK), 0)
    cols = iota2((CHUNK, CHUNK), 1)
    differ = jnp.bitwise_xor(rows, cols)
    identity = jnp.where(rows == cols, 1.0, 0.0)
    block = 1
    results = None
    while block < CHUNK:
        pick = jnp.logical_and(differ >= block, differ < 2 * block)
        parts = [jnp.where(pick, lower, 0.0) for lower in lowers]
        if block == 1:
            results = [identity - part for part in parts]
        else:
            inner = [square_three(part, result) for part, result in zip(parts, results)]
            outer = [square_three(result, mid) for mid, result in zip(inner, results)]
            results = [result - out for result, out in zip(results, outer)]
        block *= 2
    return results


def head_scalars(small, head_ref):
    decay_scale = -jnp.exp(head_ref[0:1, :])
    shifted = small + head_ref[1:2, :]
    return sigmoid(small), decay_scale * softplus(shifted), decay_scale * sigmoid(shifted)


def running_sum(values, reverse=False):
    rows = iota2((CHUNK, CHUNK), 0)
    cols = iota2((CHUNK, CHUNK), 1)
    keep = (cols >= rows) if reverse else (rows >= cols)
    ones = jnp.where(keep, 1.0, 0.0).astype(jnp.bfloat16)
    high, low = split_high(values)
    lowest = (values - high.astype(jnp.float32) - low.astype(jnp.float32)).astype(jnp.bfloat16)
    return (
        contract(ones, high, (1, 0)) + contract(ones, low, (1, 0)) + contract(ones, lowest, (1, 0))
    )


def conv_rows(window_ref, aux, taps_ref, count, lo, hi):
    total = window_ref[8 : 8 + count, lo:hi] * taps_ref[0:1, lo:hi]
    for lag in range(1, taps_ref.shape[0]):
        shifted = window_ref[8 - lag : 8 - lag + count, lo:hi] * aux[:, lag - 1 : lag]
        total = total + shifted * taps_ref[lag : lag + 1, lo:hi]
    return total


def decay_parts(cumulative, cumulative_rows, aux, segment_row, lane):
    cum_col = cumulative[:, lane : lane + 1]
    cum_row = cumulative_rows[lane : lane + 1, :]
    rows = iota2((CHUNK, CHUNK), 0)
    cols = iota2((CHUNK, CHUNK), 1)
    keep = jnp.logical_and(rows >= cols, aux[:, 5:6] == segment_row)
    matrix = jnp.where(keep, jnp.exp(jnp.minimum(cum_col - cum_row, 0.0)), 0.0)
    last = cum_col[CHUNK - 1 : CHUNK, :]
    growth = jnp.exp(cum_col) * aux[:, 3:4]
    tail = jnp.exp(last - cum_col) * aux[:, 4:5]
    carry = jnp.exp(last) * aux[CHUNK - 1 : CHUNK, 3:4]
    return matrix, growth, tail, carry


def forward_body(
    sizes,
    rank_ref,
    proj_ref,
    aux_ref,
    segment_ref,
    taps_ref,
    head_ref,
    gain_ref,
    gated_ref,
    out_ref,
    fresh_ref,
    state_ref,
    inverse_ref,
    window_ref,
    carried_ref,
):
    heads, dk, dv, chunks = sizes
    count = chunks * CHUNK
    keys, conv_cols = heads * dk, heads * (2 * dk + dv)
    gate_at, small_at = conv_cols, conv_cols + heads * dv

    @pl.when(pl.program_id(0) == 0)
    def start():
        window_ref[0:8, :] = jnp.zeros((8, conv_cols), jnp.float32)
        carried_ref[...] = jnp.zeros(carried_ref.shape, jnp.float32)

    aux = aux_ref[...]
    window_ref[8 : 8 + count, :] = proj_ref[:, :conv_cols]
    beta_all, decay_all, _ = head_scalars(proj_ref[:, small_at : small_at + LANES], head_ref)

    queries, key_rows, values = [], [], []
    for head in range(heads):
        mixed = conv_rows(window_ref, aux, taps_ref, count, head * dk, (head + 1) * dk)
        mixed = mixed * sigmoid(mixed)
        queries.append(
            mixed * (lax.rsqrt(jnp.sum(mixed * mixed, axis=1, keepdims=True) + TINY) * dk**-0.5)
        )
        mixed = conv_rows(window_ref, aux, taps_ref, count, keys + head * dk, keys + (head + 1) * dk)
        mixed = mixed * sigmoid(mixed)
        key_rows.append(mixed * lax.rsqrt(jnp.sum(mixed * mixed, axis=1, keepdims=True) + TINY))
        at = 2 * keys + head * dv
        mixed = conv_rows(window_ref, aux, taps_ref, count, at, at + dv)
        values.append(mixed * sigmoid(mixed))

    strict = iota2((CHUNK, CHUNK), 0) > iota2((CHUNK, CHUNK), 1)
    items = []
    lowers = []
    for chunk in range(chunks):
        span = slice(chunk * CHUNK, (chunk + 1) * CHUNK)
        cumulative = running_sum(decay_all[span])
        cumulative_rows = jnp.transpose(cumulative)
        for head in range(heads):
            matrix, growth, tail, carry = decay_parts(
                cumulative, cumulative_rows, aux[span], segment_ref[chunk], heads + head
            )
            beta = beta_all[span, head : head + 1]
            query, key = queries[head][span], key_rows[head][span]
            lowers.append(
                jnp.where(strict, beta * matrix * dot_three(key, key, (1, 1)), 0.0)
            )
            scores = dot_three(query, key, (1, 1)) * matrix
            items.append((span, chunk, head, beta, query, key, scores, growth, tail, carry))
    inverses = unit_inverses(lowers)
    for (span, chunk, head, beta, query, key, scores, growth, tail, carry), inverse in zip(
        items, inverses
    ):
        wide = slice(head * dv, (head + 1) * dv)
        inverse_ref[span, head * CHUNK : (head + 1) * CHUNK] = inverse
        state = carried_ref[head]
        state_ref[chunk, :, wide] = state
        right = beta * (values[head][span] - growth * dot_three(key, state))
        fresh = dot_three(inverse, right)
        fresh_ref[span, wide] = fresh
        carried_ref[head] = carry * state + dot_three(tail * key, fresh, (0, 0))
        emitted = growth * dot_three(query, state) + dot_three(scores, fresh)
        out_ref[span, wide] = emitted
        gate = proj_ref[span, gate_at + head * dv : gate_at + (head + 1) * dv]
        scale = lax.rsqrt(jnp.mean(emitted * emitted, axis=1, keepdims=True) + TINY)
        gated_ref[span, wide] = (
            emitted * scale * gain_ref[...] * (gate * sigmoid(gate))
        ).astype(jnp.bfloat16)
    window_ref[0:8, :] = proj_ref[count - 8 : count, :conv_cols]


def backward_body(
    sizes,
    rank_ref,
    proj_ref,
    before_ref,
    aux_ref,
    segment_ref,
    taps_ref,
    head_ref,
    gain_ref,
    out_ref,
    fresh_ref,
    state_ref,
    inverse_ref,
    grad_ref,
    dproj_ref,
    dtaps_ref,
    dgain_ref,
    dhead_ref,
    window_ref,
    later_ref,
    carried_ref,
):
    heads, dk, dv, chunks = sizes
    count = chunks * CHUNK
    keys, conv_cols = heads * dk, heads * (2 * dk + dv)
    gate_at, small_at = conv_cols, conv_cols + heads * dv
    lags = taps_ref.shape[0]

    @pl.when(pl.program_id(0) == 0)
    def start():
        later_ref[count : count + 8, :] = jnp.zeros((8, conv_cols), jnp.float32)
        carried_ref[...] = jnp.zeros(carried_ref.shape, jnp.float32)
        dtaps_ref[...] = jnp.zeros(dtaps_ref.shape, jnp.float32)
        dgain_ref[...] = jnp.zeros(dgain_ref.shape, jnp.float32)
        dhead_ref[...] = jnp.zeros(dhead_ref.shape, jnp.float32)

    aux = aux_ref[...]
    first = pl.program_id(0) == pl.num_programs(0) - 1
    window_ref[0:8, :] = jnp.where(first, 0.0, before_ref[:, :conv_cols])
    window_ref[8 : 8 + count, :] = proj_ref[:, :conv_cols]
    beta_all, decay_all, slope_all = head_scalars(
        proj_ref[:, small_at : small_at + LANES], head_ref
    )
    lane = iota2((CHUNK, LANES), 1)
    row_at = iota2((LANES, CHUNK), 0)
    strict = iota2((CHUNK, CHUNK), 0) > iota2((CHUNK, CHUNK), 1)

    def activated(lo, width):
        mixed = conv_rows(window_ref, aux, taps_ref, count, lo, lo + width)
        gate = sigmoid(mixed)
        return mixed * gate, gate * (1.0 + mixed * (1.0 - gate))

    for head in range(heads):
        wide = slice(head * dv, (head + 1) * dv)
        emitted = out_ref[:, wide]
        scale = lax.rsqrt(jnp.mean(emitted * emitted, axis=1, keepdims=True) + TINY)
        normed = emitted * scale
        at = gate_at + head * dv
        gate = proj_ref[:, at : at + dv]
        sig = sigmoid(gate)
        upper = grad_ref[:, wide].astype(jnp.float32)
        with_gate = upper * (gate * sig)
        dgain_ref[...] += jnp.sum((with_gate * normed).reshape(count // 8, 8, dv), axis=0)
        dproj_ref[:, at : at + dv] = (
            upper * normed * gain_ref[...] * (sig * (1.0 + gate * (1.0 - sig)))
        ).astype(jnp.bfloat16)
        dnormed = with_gate * gain_ref[...]
        dout_all = scale * (
            dnormed - normed * jnp.mean(dnormed * normed, axis=1, keepdims=True)
        )

        query_raw, query_slope = activated(head * dk, dk)
        query_scale = lax.rsqrt(jnp.sum(query_raw * query_raw, axis=1, keepdims=True) + TINY)
        query_unit = query_raw * query_scale
        key_raw, key_slope = activated(keys + head * dk, dk)
        key_scale = lax.rsqrt(jnp.sum(key_raw * key_raw, axis=1, keepdims=True) + TINY)
        key_all = key_raw * key_scale
        value_all, value_slope = activated(2 * keys + head * dv, dv)
        query_all = query_unit * dk**-0.5

        for chunk in reversed(range(chunks)):
            span = slice(chunk * CHUNK, (chunk + 1) * CHUNK)
            cumulative = running_sum(decay_all[span])
            matrix, growth, tail, carry = decay_parts(
                cumulative, jnp.transpose(cumulative), aux[span], segment_ref[chunk], heads + head
            )
            beta = beta_all[span, head : head + 1]
            query, key, value = query_all[span], key_all[span], value_all[span]
            inverse = inverse_ref[span, head * CHUNK : (head + 1) * CHUNK]
            state = state_ref[chunk, :, wide]
            fresh = fresh_ref[span, wide]
            dout = dout_all[span]
            key_products = dot_three(key, key, (1, 1)) * matrix
            scores = dot_three(query, key, (1, 1)) * matrix

            dstate = carried_ref[head]
            dfresh = dot_three(scores, dout, (0, 0)) + dot_three(tail * key, dstate)
            dright = dot_three(inverse, dfresh, (0, 0))
            carried_ref[head] = (
                carry * dstate
                + dot_three(growth * query, dout, (0, 0))
                - dot_three((growth * beta) * key, dright, (0, 0))
            )
            dscores = dot_three(dout, fresh, (1, 1))
            dlower = jnp.where(strict, -dot_three(dright, fresh, (1, 1)), 0.0)
            out_state = dot_three(dout, state, (1, 1))
            right_state = dot_three(dright, state, (1, 1))
            fresh_state = dot_three(fresh, dstate, (1, 1))
            dscores_key = dscores * matrix
            dlower_key = dlower * matrix * beta
            dquery = growth * out_state + dot_three(dscores_key, key)
            dkey = (
                tail * fresh_state
                + dot_three(dscores_key, query, (0, 0))
                - (growth * beta) * right_state
                + dot_three(dlower_key, key)
                + dot_three(dlower_key, key, (0, 0))
            )
            dvalue = beta * dright
            right_key = jnp.sum(right_state * key, axis=1, keepdims=True)
            dbeta = (
                jnp.sum(dright * value, axis=1, keepdims=True)
                - growth * right_key
                + jnp.sum(dlower * key_products, axis=1, keepdims=True)
            )
            dgrowth = jnp.sum(out_state * query, axis=1, keepdims=True) - beta * right_key
            dtail = jnp.sum(fresh_state * key, axis=1, keepdims=True)
            dcarry = jnp.sum(jnp.sum(dstate * state, axis=1, keepdims=True), axis=0, keepdims=True)
            dgap = dscores * scores + dlower * beta * key_products
            tail_term = dtail * tail
            last_term = jnp.sum(tail_term, axis=0, keepdims=True) + dcarry * carry
            is_last = iota2((CHUNK, 1), 0) == CHUNK - 1
            dcum = (
                jnp.sum(dgap, axis=1, keepdims=True)
                + dgrowth * growth
                - tail_term
                + jnp.where(is_last, last_term, 0.0)
            )
            down = jnp.sum(dgap, axis=0, keepdims=True)
            columns = jnp.transpose(jnp.where(row_at == heads + head, down, 0.0))
            ddecay = running_sum(jnp.where(lane == heads + head, dcum, 0.0) - columns, True)
            dbeta_lane = jnp.where(lane == head, dbeta, 0.0)
            dshift = ddecay * slope_all[span]
            dhead_ref[0:8, :] += jnp.sum(
                (ddecay * decay_all[span]).reshape(CHUNK // 8, 8, LANES), axis=0
            )
            dhead_ref[8:16, :] += jnp.sum(dshift.reshape(CHUNK // 8, 8, LANES), axis=0)
            sig_beta = beta_all[span]
            dsmall = dbeta_lane * (sig_beta * (1.0 - sig_beta)) + dshift
            if head == 0:
                small_parts = {} if chunk == chunks - 1 else small_parts
                small_parts[chunk] = dsmall
            else:
                small_parts[chunk] = small_parts[chunk] + dsmall

            def unit_back(grad, unit, scale_col):
                return scale_col * (grad - unit * jnp.sum(grad * unit, axis=1, keepdims=True))

            rows_at = slice(chunk * CHUNK, (chunk + 1) * CHUNK)
            later_ref[rows_at, head * dk : (head + 1) * dk] = (
                unit_back(dquery * dk**-0.5, query_unit[span], query_scale[span])
                * query_slope[span]
            )
            later_ref[rows_at, keys + head * dk : keys + (head + 1) * dk] = (
                unit_back(dkey, key, key_scale[span]) * key_slope[span]
            )
            at = 2 * keys + head * dv
            later_ref[rows_at, at : at + dv] = dvalue * value_slope[span]

    for chunk in range(chunks):
        span = slice(chunk * CHUNK, (chunk + 1) * CHUNK)
        dproj_ref[span, small_at : small_at + LANES] = small_parts[chunk].astype(jnp.bfloat16)

    block = 256
    for lo in range(0, conv_cols, block):
        hi = lo + block
        here = later_ref[0:count, lo:hi]
        total = here * taps_ref[0:1, lo:hi]
        dtaps_ref[0:8, lo:hi] += jnp.sum(
            (here * window_ref[8 : 8 + count, lo:hi]).reshape(count // 8, 8, block), axis=0
        )
        for lag in range(1, lags):
            ahead = later_ref[lag : lag + count, lo:hi] * aux[:, 5 + lag : 6 + lag]
            total = total + ahead * taps_ref[lag : lag + 1, lo:hi]
            shifted = window_ref[8 - lag : 8 - lag + count, lo:hi] * aux[:, lag - 1 : lag]
            dtaps_ref[8 * lag : 8 * lag + 8, lo:hi] += jnp.sum(
                (here * shifted).reshape(count // 8, 8, block), axis=0
            )
        dproj_ref[:, lo:hi] = total.astype(jnp.bfloat16)
    later_ref[count : count + 8, :] = later_ref[0:8, :]


FORWARD_CHUNKS = 4
BACKWARD_CHUNKS = 1


def whole_block(array):
    return pl.BlockSpec(array.shape, lambda step, rank: (0,) * array.ndim)


def turned_place(blocks, ranks):
    return lambda place, rank: lax.rem(place - rank[0] * (blocks // ranks) + blocks, blocks)


def mixer_forward(rank, proj, aux, segment_rows, taps, head_rows, gain, heads, dk, dv, ranks):
    length, width = proj.shape
    chunks = FORWARD_CHUNKS
    count = chunks * CHUNK
    steps = length // count
    conv_cols = heads * (2 * dk + dv)
    turned = turned_place(steps, ranks)
    rows = lambda cols: pl.BlockSpec((count, cols), lambda step, rank: (step, 0))
    turned_rows = lambda cols: pl.BlockSpec(
        (count, cols), lambda step, rank: (turned(step, rank), 0)
    )
    return pl.pallas_call(
        partial(forward_body, (heads, dk, dv, chunks)),
        grid_spec=pltpu.PrefetchScalarGridSpec(
            num_scalar_prefetch=1,
            grid=(steps,),
            in_specs=[
                turned_rows(width),
                rows(LANES),
                pl.BlockSpec((chunks, 1, CHUNK), lambda step, rank: (step, 0, 0)),
                whole_block(taps),
                whole_block(head_rows),
                whole_block(gain),
            ],
            out_specs=[
                turned_rows(heads * dv),
                rows(heads * dv),
                rows(heads * dv),
                pl.BlockSpec((chunks, dk, heads * dv), lambda step, rank: (step, 0, 0)),
                rows(heads * CHUNK),
            ],
            scratch_shapes=[
                pltpu.VMEM((8 + count, conv_cols), jnp.float32),
                pltpu.VMEM((heads, dk, dv), jnp.float32),
            ],
        ),
        out_shape=[
            jax.ShapeDtypeStruct((length, heads * dv), jnp.bfloat16),
            jax.ShapeDtypeStruct((length, heads * dv), jnp.float32),
            jax.ShapeDtypeStruct((length, heads * dv), jnp.float32),
            jax.ShapeDtypeStruct((length // CHUNK, dk, heads * dv), jnp.float32),
            jax.ShapeDtypeStruct((length, heads * CHUNK), jnp.float32),
        ],
        compiler_params=pltpu.CompilerParams(vmem_limit_bytes=48 * 2**20),
        cost_estimate=pl.CostEstimate(
            flops=80 * 10**9, bytes_accessed=length * width * 12, transcendentals=0
        ),
        name="mixer_forward",
    )(rank, proj, aux, segment_rows, taps, head_rows, gain)


def mixer_backward(
    rank, proj, aux, segment_rows, taps, head_rows, gain, saved, grad, heads, dk, dv, ranks
):
    length, width = proj.shape
    chunks = BACKWARD_CHUNKS
    count = chunks * CHUNK
    steps = length // count
    conv_cols = heads * (2 * dk + dv)
    out, fresh, states, inverses = saved
    place = lambda step: steps - 1 - step
    turned = turned_place(steps, ranks)
    rows = lambda cols: pl.BlockSpec((count, cols), lambda step, rank: (place(step), 0))
    turned_rows = lambda cols: pl.BlockSpec(
        (count, cols), lambda step, rank: (turned(place(step), rank), 0)
    )
    lags = taps.shape[0]
    turned_eights = turned_place(length // 8, ranks)
    before = pl.BlockSpec(
        (8, width),
        lambda step, rank: (
            turned_eights(jnp.maximum(place(step) * (count // 8) - 1, 0), rank),
            0,
        ),
    )
    whole = lambda shape: pl.BlockSpec(shape, lambda step, rank: (0, 0))
    return pl.pallas_call(
        partial(backward_body, (heads, dk, dv, chunks)),
        grid_spec=pltpu.PrefetchScalarGridSpec(
            num_scalar_prefetch=1,
            grid=(steps,),
            in_specs=[
                turned_rows(width),
                before,
                rows(LANES),
                pl.BlockSpec((chunks, 1, CHUNK), lambda step, rank: (place(step), 0, 0)),
                whole_block(taps),
                whole_block(head_rows),
                whole_block(gain),
                rows(heads * dv),
                rows(heads * dv),
                pl.BlockSpec((chunks, dk, heads * dv), lambda step, rank: (place(step), 0, 0)),
                rows(heads * CHUNK),
                turned_rows(heads * dv),
            ],
            out_specs=[
                turned_rows(width),
                whole((8 * lags, conv_cols)),
                whole((8, dv)),
                whole((16, LANES)),
            ],
            scratch_shapes=[
                pltpu.VMEM((8 + count, conv_cols), jnp.float32),
                pltpu.VMEM((8 + count, conv_cols), jnp.float32),
                pltpu.VMEM((heads, dk, dv), jnp.float32),
            ],
        ),
        out_shape=[
            jax.ShapeDtypeStruct((length, width), jnp.bfloat16),
            jax.ShapeDtypeStruct((8 * lags, conv_cols), jnp.float32),
            jax.ShapeDtypeStruct((8, dv), jnp.float32),
            jax.ShapeDtypeStruct((16, LANES), jnp.float32),
        ],
        compiler_params=pltpu.CompilerParams(vmem_limit_bytes=48 * 2**20),
        cost_estimate=pl.CostEstimate(
            flops=160 * 10**9, bytes_accessed=length * width * 16, transcendentals=0
        ),
        name="mixer_backward",
    )(
        rank, proj, proj, aux, segment_rows, taps, head_rows, gain,
        out, fresh, states, inverses, grad,
    )


def segment_columns(segments):
    length = segments.shape[0]
    blocks = segments.reshape(-1, CHUNK)

    def earlier(lag):
        return jnp.concatenate([jnp.full((lag,), -1, jnp.int32), segments[:-lag]])

    def later(lag):
        return jnp.concatenate([segments[lag:], jnp.full((lag,), -1, jnp.int32)])

    same = [segments == earlier(lag) for lag in (1, 2, 3)]
    before = earlier(1).reshape(-1, CHUNK)[:, :1]
    same.append((blocks == before).reshape(length))
    same.append((blocks == blocks[:, -1:]).reshape(length))
    columns = [one.astype(jnp.float32) for one in same] + [segments.astype(jnp.float32)]
    columns += [(segments == later(lag)).astype(jnp.float32) for lag in (1, 2, 3)]
    table = jnp.stack(columns, axis=1)
    return jnp.pad(table, ((0, 0), (0, LANES - len(columns))))


UNIT_TILE = 256


def ffn_body(
    sizes,
    rows_ref,
    cot_ref,
    gated_ref,
    gain_ref,
    *refs,
):
    ranks, tiles, spans = sizes
    weight_refs = [refs[at * 4 : at * 4 + 4] for at in range(len(spans))]
    refs = refs[4 * len(spans) :]
    output_ref, dmiddle_ref, dgated_ref, dgain_ref = refs[:4]
    grads_refs = refs[4:6]
    ffn_steps(
        ranks,
        tiles,
        spans,
        rows_ref,
        cot_ref,
        gated_ref,
        gain_ref,
        weight_refs,
        output_ref,
        dmiddle_ref,
        dgated_ref,
        dgain_ref,
        grads_refs,
        *refs[6:],
    )


def ffn_steps(
    ranks,
    tiles,
    spans,
    rows_ref,
    cot_ref,
    gated_ref,
    gain_ref,
    weight_refs,
    output_ref,
    dmiddle_ref,
    dgated_ref,
    dgain_ref,
    grads_refs,
    middle_ref,
    total_ref,
    dsecond_ref,
    second_ref,
    second_turned_ref,
    cot_turned_ref,
    dattn_ref,
    dattn_turned_ref,
):
    step = pl.program_id(0)
    tokens, width = rows_ref.shape
    begin, end = ranks, ranks + ranks * tiles
    slabs = [slice(at, at + CHUNK) for at in range(0, tokens, CHUNK)]

    def flat(ref):
        return ref[...].reshape(width, ref.shape[-1])

    @pl.when(step == 0)
    def start():
        middle_ref[...] = rows_ref[...].astype(jnp.float32)

    def attend(w_out_ref):
        middle_ref[...] += contract(gated_ref[...], flat(w_out_ref), (1, 1))

    for (low, high), held in zip(spans, weight_refs):
        pl.when(jnp.logical_and(step >= low, step < high))(partial(attend, held[0]))

    @pl.when(step == begin)
    def second_norm():
        for slab in slabs:
            middle = middle_ref[slab, :]
            scale = lax.rsqrt(jnp.mean(middle * middle, axis=1, keepdims=True) + TINY)
            second = middle * scale * gain_ref[...]
            second_ref[slab, :] = second.astype(jnp.bfloat16)
            second_turned_ref[:, slab] = jnp.transpose(second).astype(jnp.bfloat16)
            cot_turned_ref[:, slab] = jnp.transpose(
                cot_ref[slab, :].astype(jnp.float32)
            ).astype(jnp.bfloat16)
        total_ref[...] = jnp.zeros(total_ref.shape, jnp.float32)
        dsecond_ref[...] = jnp.zeros(dsecond_ref.shape, jnp.float32)

    def units(w_gate_ref, w_up_ref, w_down_ref, grads_ref):
        w_gate, w_up, w_down = flat(w_gate_ref), flat(w_up_ref), flat(w_down_ref)
        second = second_ref[...]
        gate = contract(second, w_gate, (1, 0))
        up = contract(second, w_up, (1, 0))
        dhidden = contract(cot_ref[...], w_down, (1, 0))
        sig = sigmoid(gate)
        active = gate * sig
        hidden = (active * up).astype(jnp.bfloat16)
        dgate = (dhidden * up * (sig * (1.0 + gate * (1.0 - sig)))).astype(jnp.bfloat16)
        dup = (dhidden * active).astype(jnp.bfloat16)
        total_ref[...] += contract(hidden, w_down, (1, 1))
        dsecond_ref[...] += contract(dgate, w_gate, (1, 1)) + contract(dup, w_up, (1, 1))
        turned = second_turned_ref[...]
        tile = gate.shape[1]
        grads_ref[:, :tile] = contract(turned, dgate, (1, 0)).astype(jnp.bfloat16)
        grads_ref[:, tile : 2 * tile] = contract(turned, dup, (1, 0)).astype(jnp.bfloat16)
        grads_ref[:, 2 * tile :] = contract(cot_turned_ref[...], hidden, (1, 0)).astype(
            jnp.bfloat16
        )

    for (low, high), held in zip(spans, weight_refs):
        grads_ref = grads_refs[0 if low == 0 else 1]
        pl.when(jnp.logical_and(step >= begin + low * tiles, step < begin + high * tiles))(
            partial(units, *held[1:], grads_ref)
        )

    @pl.when(step == end)
    def second_norm_back():
        dgain_ref[...] = jnp.zeros(dgain_ref.shape, jnp.float32)
        for slab in slabs:
            middle = middle_ref[slab, :]
            output_ref[slab, :] = (middle + total_ref[slab, :]).astype(jnp.bfloat16)
            scale = lax.rsqrt(jnp.mean(middle * middle, axis=1, keepdims=True) + TINY)
            normed = middle * scale
            dsecond = dsecond_ref[slab, :]
            dgain_ref[...] += jnp.sum((dsecond * normed).reshape(CHUNK // 8, 8, width), axis=0)
            scaled = dsecond * gain_ref[...]
            dmiddle = cot_ref[slab, :].astype(jnp.float32) + scale * (
                scaled - normed * jnp.mean(scaled * normed, axis=1, keepdims=True)
            )
            dmiddle_ref[slab, :] = dmiddle
            dattn_ref[slab, :] = dmiddle.astype(jnp.bfloat16)
            dattn_turned_ref[:, slab] = jnp.transpose(dmiddle).astype(jnp.bfloat16)

    def attend_back(w_out_ref):
        dgated_ref[...] = contract(dattn_ref[...], flat(w_out_ref), (1, 0)).astype(
            dgated_ref.dtype
        )
        cols = gated_ref.shape[1]
        last_ref = grads_refs[-1]
        last_ref[:, :cols] = contract(dattn_turned_ref[...], gated_ref[...], (1, 0)).astype(
            jnp.bfloat16
        )
        last_ref[:, cols:] = jnp.zeros((last_ref.shape[0], last_ref.shape[1] - cols), jnp.bfloat16)

    for (low, high), held in zip(spans, weight_refs):
        pl.when(jnp.logical_and(step >= end + low, step < end + high))(
            partial(attend_back, held[0])
        )


def ffn_block(rows, cot, gated, weights, spans, gain, value_cols, unit_cols):
    tokens, width = rows.shape
    ranks = spans[-1][1]
    grad_spans = [(0, 1), (1, ranks)]
    tiles = unit_cols // UNIT_TILE
    begin, end = ranks, ranks + ranks * tiles
    group = 3 * UNIT_TILE

    def edge(step):
        return jnp.where(step < end, jnp.minimum(step, ranks - 1), step - end)

    def out_spec(array, low, high):
        return pl.BlockSpec(
            (array.shape[0], 1, array.shape[2], value_cols),
            lambda step: (0, jnp.clip(edge(step) - low, 0, high - low - 1), 0, 0),
        )

    def tile_at(step, low, high):
        return jnp.clip(step - begin - low * tiles, 0, (high - low) * tiles - 1)

    def unit_spec(array, low, high, kind):
        first = value_cols // UNIT_TILE + kind * tiles

        def place(step):
            tile = tile_at(step, low, high)
            return (0, tile // tiles, 0, first + lax.rem(tile, tiles))

        return pl.BlockSpec((array.shape[0], 1, array.shape[2], UNIT_TILE), place)

    def grads_at(step, low, high):
        place = tile_at(step, low, high)
        return jnp.where(step < end, place, place + 1 + step - end) if high == ranks else place

    whole = lambda shape: pl.BlockSpec(shape, lambda step: (0,) * len(shape))
    bf, f32 = jnp.bfloat16, jnp.float32
    weight_specs, weight_args = [], []
    for array, (low, high) in zip(weights, spans):
        weight_specs.append(out_spec(array, low, high))
        weight_specs += [unit_spec(array, low, high, kind) for kind in range(3)]
        weight_args += [array] * 4
    late = lambda step: (0, jnp.maximum(step - end, 0))
    return pl.pallas_call(
        partial(ffn_body, (ranks, tiles, tuple(spans))),
        grid=(end + ranks,),
        in_specs=[
            whole(rows.shape),
            whole(cot.shape),
            pl.BlockSpec((tokens, value_cols), lambda step: (0, edge(step))),
            whole(gain.shape),
            *weight_specs,
        ],
        out_specs=[
            whole(rows.shape),
            whole(rows.shape),
            pl.BlockSpec((tokens, value_cols), late),
            whole((8, width)),
        ]
        + [
            pl.BlockSpec(
                (width, group), lambda step, low=low, high=high: (0, grads_at(step, low, high))
            )
            for low, high in grad_spans
        ],
        scratch_shapes=[
            pltpu.VMEM((tokens, width), f32),
            pltpu.VMEM((tokens, width), f32),
            pltpu.VMEM((tokens, width), f32),
            pltpu.VMEM((tokens, width), bf),
            pltpu.VMEM((width, tokens), bf),
            pltpu.VMEM((width, tokens), bf),
            pltpu.VMEM((tokens, width), bf),
            pltpu.VMEM((width, tokens), bf),
        ],
        out_shape=[
            jax.ShapeDtypeStruct(rows.shape, bf),
            jax.ShapeDtypeStruct(rows.shape, f32),
            jax.ShapeDtypeStruct((tokens, ranks * value_cols), bf),
            jax.ShapeDtypeStruct((8, width), f32),
        ]
        + [
            jax.ShapeDtypeStruct(
                (width, ((high - low) * tiles + (ranks if high == ranks else 0)) * group), bf
            )
            for low, high in grad_spans
        ],
        compiler_params=pltpu.CompilerParams(vmem_limit_bytes=60 * 2**20),
        cost_estimate=pl.CostEstimate(
            flops=35 * 10**9, bytes_accessed=60 * 10**6, transcendentals=0
        ),
        name="ffn_block",
    )(rows, cot, gated, gain, *weight_args)


def rms_back(grad, gain, normed, scale):
    scaled = grad * gain
    return scale * (scaled - normed * jnp.mean(scaled * normed, axis=-1, keepdims=True))


def padded(array, width):
    return jnp.pad(array, ((0, 0), (0, width - array.shape[1])))


def product(left, right, left_dim, right_dim):
    return lax.dot_general(
        left, right, (((left_dim,), (right_dim,)), ((), ())), preferred_element_type=jnp.float32
    )


def up_to(size, unit):
    return -(-size // unit) * unit


def fetched(block, ahead, ranks):
    return lax.ppermute(block, "tensor", [((i + ahead) % ranks, i) for i in range(ranks)])


def exchanged(blocks):
    ranks = len(blocks)
    result = [blocks[0]] + [None] * (ranks - 1)
    for ahead in range(1, ranks):
        result[ranks - ahead] = lax.ppermute(
            blocks[ahead], "tensor", [(i, (i + ahead) % ranks) for i in range(ranks)]
        )
    return result


def stacked_body(*refs):
    for at, ref in enumerate(refs[1:-1]):
        refs[-1][at] = ref[...]


def stacked_after(blocks, earlier):
    return pl.pallas_call(
        stacked_body,
        in_specs=[pl.BlockSpec(memory_space=pl.ANY)]
        + [pl.BlockSpec(memory_space=pltpu.VMEM)] * len(blocks),
        out_specs=pl.BlockSpec(memory_space=pltpu.VMEM),
        out_shape=jax.ShapeDtypeStruct((len(blocks), *blocks[0].shape), blocks[0].dtype),
        name="stacked_after",
    )(earlier, *blocks)


def summed_over(vector, axis):
    size = lax.axis_size(axis)
    apart = 1
    while apart < size:
        vector = vector + lax.ppermute(vector, axis, [(i, i ^ apart) for i in range(size)])
        apart *= 2
    return vector


def shards(
    layer_input,
    segments,
    norm_gain,
    w_query,
    w_key,
    w_value,
    w_outgate,
    w_beta,
    w_decay,
    conv_query,
    conv_key,
    conv_value,
    decay_log,
    decay_bias,
    out_gain,
    w_out,
    ffn_gain,
    w_gate,
    w_up,
    w_down,
    cotangent,
):
    tensor_rank = lax.axis_index("tensor")
    ranks = lax.axis_size("tensor")
    key_cols, value_cols, heads = w_query.shape[1], w_value.shape[1], w_beta.shape[1]
    dk, dv = key_cols // heads, value_cols // heads
    units = w_gate.shape[1]
    unit_cols = up_to(units, UNIT_TILE)
    tokens = layer_input.shape[0]
    conv_cols = 2 * key_cols + value_cols
    gate_at, small_at = conv_cols, conv_cols + value_cols

    joined = lax.all_gather(
        padded(
            jnp.concatenate([w_query, w_key, w_value, w_outgate, w_beta, w_decay], axis=1),
            small_at + LANES,
        ),
        "dp",
        axis=0,
        tiled=True,
    )
    rest_shard = jnp.concatenate(
        [w_out.T, padded(w_gate, unit_cols), padded(w_up, unit_cols), padded(w_down.T, unit_cols)],
        axis=1,
    )
    rest_shard = with_layout_constraint(rest_shard, Layout(major_to_minor=(0, 1)))

    near_rest = lax.all_gather(rest_shard[None], "dp")

    residual = layer_input.astype(jnp.float32)
    first_scale = lax.rsqrt(jnp.mean(residual * residual, axis=-1, keepdims=True) + TINY)
    first_normed = residual * first_scale
    first = (first_normed * norm_gain).astype(jnp.bfloat16)
    mixer_blocks = [first] + [fetched(first, ahead, ranks) for ahead in range(1, ranks)]
    mixer_rows = jnp.concatenate(mixer_blocks, axis=0)
    projected = product(mixer_rows, joined, 1, 0)

    rest_shard, _ = lax.optimization_barrier((rest_shard, mixer_blocks))
    far = [fetched(rest_shard, ahead, ranks) for ahead in range(1, ranks)]

    def local(array, width):
        return lax.dynamic_slice_in_dim(array, tensor_rank * width, width, array.ndim - 1)

    taps = jnp.concatenate(
        [local(conv_query, key_cols), local(conv_key, key_cols), local(conv_value, value_cols)],
        axis=1,
    )
    head_rows = jnp.pad(
        jnp.stack([local(decay_log, heads), local(decay_bias, heads)]),
        ((0, 6), (heads, LANES - 2 * heads)),
    )
    gain_row = out_gain[None, :]
    aux = segment_columns(segments)
    segment_rows = segments.astype(jnp.float32).reshape(-1, 1, CHUNK)
    rank = tensor_rank.astype(jnp.int32).reshape(1)
    ahead, projected = lax.optimization_barrier((far[0], projected))
    next_rest = lax.all_gather(ahead[None], "dp")
    gated, *saved = mixer_forward(
        rank, projected, aux, segment_rows, taps, head_rows, gain_row, heads, dk, dv, ranks
    )

    def token_blocks(array):
        return [array[at * tokens : (at + 1) * tokens] for at in range(ranks)]

    far_rest = lax.all_gather(stacked_after(far[1:], gated), "dp")
    gated_rows = jnp.concatenate(exchanged(token_blocks(gated)), axis=1)
    spans = [(0, 1), (1, 2), (2, ranks)]
    layer_output, grad_middle, grad_gated, dffn, near_grads, far_grads = ffn_block(
        layer_input,
        cotangent,
        gated_rows,
        [near_rest, next_rest, far_rest],
        spans,
        ffn_gain[None, :],
        value_cols,
        unit_cols,
    )

    def scattered(array):
        return lax.psum_scatter(array, "dp", scatter_dimension=0, tiled=True)

    summed_far = scattered(far_grads)
    grad_gated_rows = jnp.concatenate(
        exchanged(
            [grad_gated[:, at * value_cols : (at + 1) * value_cols] for at in range(ranks)]
        ),
        axis=0,
    )
    grad_proj, dtaps, dgain, dhead = mixer_backward(
        rank,
        projected,
        aux,
        segment_rows,
        taps,
        head_rows,
        gain_row,
        saved,
        grad_gated_rows,
        heads,
        dk,
        dv,
        ranks,
    )
    back_first = [
        product(block, joined, 1, 1).astype(jnp.bfloat16) for block in token_blocks(grad_proj)
    ]
    grad_proj, _ = lax.optimization_barrier((grad_proj, back_first))
    grad_joined = product(mixer_rows, grad_proj, 0, 0)
    received_first = exchanged(back_first)
    grad_norm_gain = jnp.sum(joined.astype(jnp.float32) * grad_joined, axis=1) / norm_gain

    group = 3 * UNIT_TILE
    tiles = unit_cols // UNIT_TILE
    span_cols = tiles * group
    grad_joined_low = grad_joined.astype(jnp.bfloat16)
    near_grads, summed_far = lax.optimization_barrier(
        (jnp.concatenate([near_grads, grad_joined_low], axis=1), summed_far)
    )
    summed_near = scattered(near_grads)
    summed_joined = summed_near[:, span_cols:].astype(jnp.float32)
    out_at = (ranks - 1) * span_cols
    outs_for = [
        summed_far[:, out_at + at * group : out_at + at * group + value_cols]
        for at in range(ranks)
    ]
    rest_sends = [outs_for[0]] + [
        jnp.concatenate(
            [summed_far[:, at * span_cols : (at + 1) * span_cols], outs_for[at + 1]], axis=1
        )
        for at in range(ranks - 1)
    ]

    lags = taps.shape[0]
    mine = jnp.concatenate(
        [
            jnp.sum(dtaps.reshape(lags, 8, conv_cols), axis=1).reshape(-1),
            jnp.sum(dhead[0:8], axis=0)[heads : 2 * heads],
            jnp.sum(dhead[8:16], axis=0)[heads : 2 * heads],
        ]
    )
    placed = jnp.where((jnp.arange(ranks) == tensor_rank)[:, None], mine[None, :], 0.0)
    vector = jnp.concatenate(
        [grad_norm_gain, jnp.sum(dffn, axis=0), jnp.sum(dgain, axis=0), placed.reshape(-1)]
    )
    received_first, rest_sends, vector = lax.optimization_barrier(
        (received_first, rest_sends, vector)
    )
    small = summed_over(summed_over(vector, "dp"), "tensor")
    received_rest = exchanged(rest_sends)
    owned = summed_near[:, :span_cols].astype(jnp.float32) + sum(
        part[:, :span_cols].astype(jnp.float32) for part in received_rest[1:]
    )
    owned_out = received_rest[0].astype(jnp.float32) + sum(
        part[:, span_cols:].astype(jnp.float32) for part in received_rest[1:]
    )
    by_kind = [
        jnp.concatenate(
            [
                owned[:, tile * group + kind * UNIT_TILE : tile * group + (kind + 1) * UNIT_TILE]
                for tile in range(tiles)
            ],
            axis=1,
        )[:, :units]
        for kind in range(3)
    ]
    grad_first = sum(part.astype(jnp.float32) for part in received_first)
    grad_input = grad_middle + rms_back(grad_first, norm_gain, first_normed, first_scale)
    width = norm_gain.shape[0]
    sections = small[2 * width + dv :].reshape(ranks, -1)
    taps_all = sections[:, : lags * conv_cols].reshape(ranks, lags, conv_cols).transpose(1, 0, 2)
    logs_all = sections[:, lags * conv_cols :]

    def columns(lo, hi):
        return summed_joined[:, lo:hi]

    return (
        layer_output,
        grad_input,
        small[:width],
        columns(0, key_cols),
        columns(key_cols, 2 * key_cols),
        columns(2 * key_cols, conv_cols),
        columns(gate_at, small_at),
        columns(small_at, small_at + heads),
        columns(small_at + heads, small_at + 2 * heads),
        taps_all[:, :, :key_cols].reshape(lags, -1),
        taps_all[:, :, key_cols : 2 * key_cols].reshape(lags, -1),
        taps_all[:, :, 2 * key_cols :].reshape(lags, -1),
        logs_all[:, :heads].reshape(-1),
        logs_all[:, heads:].reshape(-1),
        small[2 * width : 2 * width + dv],
        owned_out.T,
        small[width : 2 * width],
        by_kind[0],
        by_kind[1],
        by_kind[2].T,
    )


def solution(mesh):
    in_specs = (
        P(("dp", "tensor"), None),
        P("dp"),
        P(),
        P("dp", "tensor"),
        P("dp", "tensor"),
        P("dp", "tensor"),
        P("dp", "tensor"),
        P("dp", "tensor"),
        P("dp", "tensor"),
        P(),
        P(),
        P(),
        P(),
        P(),
        P(),
        P("tensor", "dp"),
        P(),
        P("dp", "tensor"),
        P("dp", "tensor"),
        P("tensor", "dp"),
        P(("dp", "tensor"), None),
    )
    out_specs = (
        P(("dp", "tensor"), None),
        P(("dp", "tensor"), None),
        P(),
        P("dp", "tensor"),
        P("dp", "tensor"),
        P("dp", "tensor"),
        P("dp", "tensor"),
        P("dp", "tensor"),
        P("dp", "tensor"),
        P(),
        P(),
        P(),
        P(),
        P(),
        P(),
        P("tensor", "dp"),
        P(),
        P("dp", "tensor"),
        P("dp", "tensor"),
        P("tensor", "dp"),
    )
    return jax.shard_map(shards, mesh=mesh, in_specs=in_specs, out_specs=out_specs, check_vma=False)
```

```python
from functools import partial

import jax
import jax.numpy as jnp
from jax import lax
from jax.experimental import pallas as pl
from jax.experimental.layout import Layout, with_layout_constraint
from jax.experimental.pallas import tpu as pltpu
from jax.sharding import PartitionSpec as P

CHUNK = 128
TINY = 1e-06
LANES = 128


def split_high(values):
    high = values.astype(jnp.bfloat16)
    return high, (values - high.astype(jnp.float32)).astype(jnp.bfloat16)


def contract(left, right, dims):
    return lax.dot_general(
        left, right, ((dims[:1], dims[1:]), ((), ())), preferred_element_type=jnp.float32
    )


def dot_one(left, right, dims=(1, 0)):
    return contract(left.astype(jnp.bfloat16), right.astype(jnp.bfloat16), dims)


def dot_three(left, right, dims=(1, 0)):
    left_high, left_low = split_high(left)
    right_high, right_low = split_high(right)
    return (
        contract(left_high, right_high, dims)
        + contract(left_high, right_low, dims)
        + contract(left_low, right_high, dims)
    )


def square_three(left, right):
    left_high, left_low = split_high(left)
    right_high, right_low = split_high(right)
    wide_left = jnp.concatenate([left_high, left_low], axis=1)
    row = jnp.concatenate([right_high, right_low], axis=1)
    product = contract(wide_left, jnp.concatenate([row, row], axis=0), (1, 0))
    width = right.shape[1]
    return product[:, :width] + product[:, width:]


def iota2(shape, axis):
    return lax.broadcasted_iota(jnp.int32, shape, axis)


def sigmoid(values):
    return 1.0 / (1.0 + jnp.exp(-values))


def softplus(values):
    return jnp.maximum(values, 0.0) + jnp.log1p(jnp.exp(-jnp.abs(values)))


def unit_inverses(lowers):
    rows = iota2((CHUNK, CHUNK), 0)
    cols = iota2((CHUNK, CHUNK), 1)
    differ = jnp.bitwise_xor(rows, cols)
    identity = jnp.where(rows == cols, 1.0, 0.0)
    block = 1
    results = None
    while block < CHUNK:
        pick = jnp.logical_and(differ >= block, differ < 2 * block)
        parts = [jnp.where(pick, lower, 0.0) for lower in lowers]
        if block == 1:
            results = [identity - part for part in parts]
        else:
            inner = [square_three(part, result) for part, result in zip(parts, results)]
            outer = [square_three(result, mid) for mid, result in zip(inner, results)]
            results = [result - out for result, out in zip(results, outer)]
        block *= 2
    return results


def head_scalars(small, head_ref):
    decay_scale = -jnp.exp(head_ref[0:1, :])
    shifted = small + head_ref[1:2, :]
    return sigmoid(small), decay_scale * softplus(shifted), decay_scale * sigmoid(shifted)


def running_sum(values, reverse=False):
    rows = iota2((CHUNK, CHUNK), 0)
    cols = iota2((CHUNK, CHUNK), 1)
    keep = (cols >= rows) if reverse else (rows >= cols)
    ones = jnp.where(keep, 1.0, 0.0).astype(jnp.bfloat16)
    high, low = split_high(values)
    lowest = (values - high.astype(jnp.float32) - low.astype(jnp.float32)).astype(jnp.bfloat16)
    return (
        contract(ones, high, (1, 0)) + contract(ones, low, (1, 0)) + contract(ones, lowest, (1, 0))
    )


def conv_rows(window_ref, aux, taps_ref, count, lo, hi):
    total = window_ref[8 : 8 + count, lo:hi] * taps_ref[0:1, lo:hi]
    for lag in range(1, taps_ref.shape[0]):
        shifted = window_ref[8 - lag : 8 - lag + count, lo:hi] * aux[:, lag - 1 : lag]
        total = total + shifted * taps_ref[lag : lag + 1, lo:hi]
    return total


def decay_parts(cumulative, cumulative_rows, aux, segment_row, lane):
    cum_col = cumulative[:, lane : lane + 1]
    cum_row = cumulative_rows[lane : lane + 1, :]
    rows = iota2((CHUNK, CHUNK), 0)
    cols = iota2((CHUNK, CHUNK), 1)
    keep = jnp.logical_and(rows >= cols, aux[:, 5:6] == segment_row)
    matrix = jnp.where(keep, jnp.exp(jnp.minimum(cum_col - cum_row, 0.0)), 0.0)
    last = cum_col[CHUNK - 1 : CHUNK, :]
    growth = jnp.exp(cum_col) * aux[:, 3:4]
    tail = jnp.exp(last - cum_col) * aux[:, 4:5]
    carry = jnp.exp(last) * aux[CHUNK - 1 : CHUNK, 3:4]
    return matrix, growth, tail, carry


def forward_body(
    sizes,
    rank_ref,
    proj_ref,
    aux_ref,
    segment_ref,
    taps_ref,
    head_ref,
    gain_ref,
    gated_ref,
    out_ref,
    fresh_ref,
    state_ref,
    inverse_ref,
    window_ref,
    carried_ref,
):
    heads, dk, dv, chunks = sizes
    count = chunks * CHUNK
    keys, conv_cols = heads * dk, heads * (2 * dk + dv)
    gate_at, small_at = conv_cols, conv_cols + heads * dv

    @pl.when(pl.program_id(0) == 0)
    def start():
        window_ref[0:8, :] = jnp.zeros((8, conv_cols), jnp.float32)
        carried_ref[...] = jnp.zeros(carried_ref.shape, jnp.float32)

    aux = aux_ref[...]
    window_ref[8 : 8 + count, :] = proj_ref[:, :conv_cols]
    beta_all, decay_all, _ = head_scalars(proj_ref[:, small_at : small_at + LANES], head_ref)

    queries, key_rows, values = [], [], []
    for head in range(heads):
        mixed = conv_rows(window_ref, aux, taps_ref, count, head * dk, (head + 1) * dk)
        mixed = mixed * sigmoid(mixed)
        queries.append(
            mixed * (lax.rsqrt(jnp.sum(mixed * mixed, axis=1, keepdims=True) + TINY) * dk**-0.5)
        )
        mixed = conv_rows(window_ref, aux, taps_ref, count, keys + head * dk, keys + (head + 1) * dk)
        mixed = mixed * sigmoid(mixed)
        key_rows.append(mixed * lax.rsqrt(jnp.sum(mixed * mixed, axis=1, keepdims=True) + TINY))
        at = 2 * keys + head * dv
        mixed = conv_rows(window_ref, aux, taps_ref, count, at, at + dv)
        values.append(mixed * sigmoid(mixed))

    strict = iota2((CHUNK, CHUNK), 0) > iota2((CHUNK, CHUNK), 1)
    items = []
    lowers = []
    for chunk in range(chunks):
        span = slice(chunk * CHUNK, (chunk + 1) * CHUNK)
        cumulative = running_sum(decay_all[span])
        cumulative_rows = jnp.transpose(cumulative)
        for head in range(heads):
            matrix, growth, tail, carry = decay_parts(
                cumulative, cumulative_rows, aux[span], segment_ref[chunk], heads + head
            )
            beta = beta_all[span, head : head + 1]
            query, key = queries[head][span], key_rows[head][span]
            lowers.append(
                jnp.where(strict, beta * matrix * dot_three(key, key, (1, 1)), 0.0)
            )
            scores = dot_three(query, key, (1, 1)) * matrix
            items.append((span, chunk, head, beta, query, key, scores, growth, tail, carry))
    inverses = unit_inverses(lowers)
    for (span, chunk, head, beta, query, key, scores, growth, tail, carry), inverse in zip(
        items, inverses
    ):
        wide = slice(head * dv, (head + 1) * dv)
        inverse_ref[span, head * CHUNK : (head + 1) * CHUNK] = inverse
        state = carried_ref[head]
        state_ref[chunk, :, wide] = state
        right = beta * (values[head][span] - growth * dot_three(key, state))
        fresh = dot_three(inverse, right)
        fresh_ref[span, wide] = fresh
        carried_ref[head] = carry * state + dot_three(tail * key, fresh, (0, 0))
        emitted = growth * dot_three(query, state) + dot_three(scores, fresh)
        out_ref[span, wide] = emitted
        gate = proj_ref[span, gate_at + head * dv : gate_at + (head + 1) * dv]
        scale = lax.rsqrt(jnp.mean(emitted * emitted, axis=1, keepdims=True) + TINY)
        gated_ref[span, wide] = (
            emitted * scale * gain_ref[...] * (gate * sigmoid(gate))
        ).astype(jnp.bfloat16)
    window_ref[0:8, :] = proj_ref[count - 8 : count, :conv_cols]


def backward_body(
    sizes,
    held,
    rank_ref,
    proj_ref,
    before_ref,
    aux_ref,
    segment_ref,
    taps_ref,
    head_ref,
    gain_ref,
    out_ref,
    fresh_ref,
    state_ref,
    inverse_ref,
    grad_ref,
    later_in_ref,
    carried_in_ref,
    *refs,
):
    dproj_ref, dtaps_ref, dgain_ref, dhead_ref, later_out_ref, carried_ref = refs[held : held + 6]
    window_ref, later_ref = refs[held + 6 :]
    heads, dk, dv, chunks, top = sizes
    count = chunks * CHUNK
    keys, conv_cols = heads * dk, heads * (2 * dk + dv)
    gate_at, small_at = conv_cols, conv_cols + heads * dv
    lags = taps_ref.shape[0]

    @pl.when(pl.program_id(0) == 0)
    def start():
        later_ref[count : count + 8, :] = later_in_ref[...]
        carried_ref[...] = carried_in_ref[...]
        dtaps_ref[...] = jnp.zeros(dtaps_ref.shape, jnp.float32)
        dgain_ref[...] = jnp.zeros(dgain_ref.shape, jnp.float32)
        dhead_ref[...] = jnp.zeros(dhead_ref.shape, jnp.float32)

    aux = aux_ref[...]
    first = pl.program_id(0) == top
    window_ref[0:8, :] = jnp.where(first, 0.0, before_ref[:, :conv_cols])
    window_ref[8 : 8 + count, :] = proj_ref[:, :conv_cols]
    beta_all, decay_all, slope_all = head_scalars(
        proj_ref[:, small_at : small_at + LANES], head_ref
    )
    lane = iota2((CHUNK, LANES), 1)
    row_at = iota2((LANES, CHUNK), 0)
    strict = iota2((CHUNK, CHUNK), 0) > iota2((CHUNK, CHUNK), 1)

    def activated(lo, width):
        mixed = conv_rows(window_ref, aux, taps_ref, count, lo, lo + width)
        gate = sigmoid(mixed)
        return mixed * gate, gate * (1.0 + mixed * (1.0 - gate))

    for head in range(heads):
        wide = slice(head * dv, (head + 1) * dv)
        emitted = out_ref[:, wide]
        scale = lax.rsqrt(jnp.mean(emitted * emitted, axis=1, keepdims=True) + TINY)
        normed = emitted * scale
        at = gate_at + head * dv
        gate = proj_ref[:, at : at + dv]
        sig = sigmoid(gate)
        upper = grad_ref[:, wide].astype(jnp.float32)
        with_gate = upper * (gate * sig)
        dgain_ref[...] += jnp.sum((with_gate * normed).reshape(count // 8, 8, dv), axis=0)
        dproj_ref[:, at : at + dv] = (
            upper * normed * gain_ref[...] * (sig * (1.0 + gate * (1.0 - sig)))
        ).astype(jnp.bfloat16)
        dnormed = with_gate * gain_ref[...]
        dout_all = scale * (
            dnormed - normed * jnp.mean(dnormed * normed, axis=1, keepdims=True)
        )

        query_raw, query_slope = activated(head * dk, dk)
        query_scale = lax.rsqrt(jnp.sum(query_raw * query_raw, axis=1, keepdims=True) + TINY)
        query_unit = query_raw * query_scale
        key_raw, key_slope = activated(keys + head * dk, dk)
        key_scale = lax.rsqrt(jnp.sum(key_raw * key_raw, axis=1, keepdims=True) + TINY)
        key_all = key_raw * key_scale
        value_all, value_slope = activated(2 * keys + head * dv, dv)
        query_all = query_unit * dk**-0.5

        for chunk in reversed(range(chunks)):
            span = slice(chunk * CHUNK, (chunk + 1) * CHUNK)
            cumulative = running_sum(decay_all[span])
            matrix, growth, tail, carry = decay_parts(
                cumulative, jnp.transpose(cumulative), aux[span], segment_ref[chunk], heads + head
            )
            beta = beta_all[span, head : head + 1]
            query, key, value = query_all[span], key_all[span], value_all[span]
            inverse = inverse_ref[span, head * CHUNK : (head + 1) * CHUNK]
            state = state_ref[chunk, :, wide]
            fresh = fresh_ref[span, wide]
            dout = dout_all[span]
            key_products = dot_three(key, key, (1, 1)) * matrix
            scores = dot_three(query, key, (1, 1)) * matrix

            dstate = carried_ref[head]
            dfresh = dot_three(scores, dout, (0, 0)) + dot_three(tail * key, dstate)
            dright = dot_three(inverse, dfresh, (0, 0))
            carried_ref[head] = (
                carry * dstate
                + dot_three(growth * query, dout, (0, 0))
                - dot_three((growth * beta) * key, dright, (0, 0))
            )
            dscores = dot_three(dout, fresh, (1, 1))
            dlower = jnp.where(strict, -dot_three(dright, fresh, (1, 1)), 0.0)
            out_state = dot_three(dout, state, (1, 1))
            right_state = dot_three(dright, state, (1, 1))
            fresh_state = dot_three(fresh, dstate, (1, 1))
            dscores_key = dscores * matrix
            dlower_key = dlower * matrix * beta
            dquery = growth * out_state + dot_three(dscores_key, key)
            dkey = (
                tail * fresh_state
                + dot_three(dscores_key, query, (0, 0))
                - (growth * beta) * right_state
                + dot_three(dlower_key, key)
                + dot_three(dlower_key, key, (0, 0))
            )
            dvalue = beta * dright
            right_key = jnp.sum(right_state * key, axis=1, keepdims=True)
            dbeta = (
                jnp.sum(dright * value, axis=1, keepdims=True)
                - growth * right_key
                + jnp.sum(dlower * key_products, axis=1, keepdims=True)
            )
            dgrowth = jnp.sum(out_state * query, axis=1, keepdims=True) - beta * right_key
            dtail = jnp.sum(fresh_state * key, axis=1, keepdims=True)
            dcarry = jnp.sum(jnp.sum(dstate * state, axis=1, keepdims=True), axis=0, keepdims=True)
            dgap = dscores * scores + dlower * beta * key_products
            tail_term = dtail * tail
            last_term = jnp.sum(tail_term, axis=0, keepdims=True) + dcarry * carry
            is_last = iota2((CHUNK, 1), 0) == CHUNK - 1
            dcum = (
                jnp.sum(dgap, axis=1, keepdims=True)
                + dgrowth * growth
                - tail_term
                + jnp.where(is_last, last_term, 0.0)
            )
            down = jnp.sum(dgap, axis=0, keepdims=True)
            columns = jnp.transpose(jnp.where(row_at == heads + head, down, 0.0))
            ddecay = running_sum(jnp.where(lane == heads + head, dcum, 0.0) - columns, True)
            dbeta_lane = jnp.where(lane == head, dbeta, 0.0)
            dshift = ddecay * slope_all[span]
            dhead_ref[0:8, :] += jnp.sum(
                (ddecay * decay_all[span]).reshape(CHUNK // 8, 8, LANES), axis=0
            )
            dhead_ref[8:16, :] += jnp.sum(dshift.reshape(CHUNK // 8, 8, LANES), axis=0)
            sig_beta = beta_all[span]
            dsmall = dbeta_lane * (sig_beta * (1.0 - sig_beta)) + dshift
            if head == 0:
                small_parts = {} if chunk == chunks - 1 else small_parts
                small_parts[chunk] = dsmall
            else:
                small_parts[chunk] = small_parts[chunk] + dsmall

            def unit_back(grad, unit, scale_col):
                return scale_col * (grad - unit * jnp.sum(grad * unit, axis=1, keepdims=True))

            rows_at = slice(chunk * CHUNK, (chunk + 1) * CHUNK)
            later_ref[rows_at, head * dk : (head + 1) * dk] = (
                unit_back(dquery * dk**-0.5, query_unit[span], query_scale[span])
                * query_slope[span]
            )
            later_ref[rows_at, keys + head * dk : keys + (head + 1) * dk] = (
                unit_back(dkey, key, key_scale[span]) * key_slope[span]
            )
            at = 2 * keys + head * dv
            later_ref[rows_at, at : at + dv] = dvalue * value_slope[span]

    for chunk in range(chunks):
        span = slice(chunk * CHUNK, (chunk + 1) * CHUNK)
        dproj_ref[span, small_at : small_at + LANES] = small_parts[chunk].astype(jnp.bfloat16)

    block = 256
    for lo in range(0, conv_cols, block):
        hi = lo + block
        here = later_ref[0:count, lo:hi]
        total = here * taps_ref[0:1, lo:hi]
        dtaps_ref[0:8, lo:hi] += jnp.sum(
            (here * window_ref[8 : 8 + count, lo:hi]).reshape(count // 8, 8, block), axis=0
        )
        for lag in range(1, lags):
            ahead = later_ref[lag : lag + count, lo:hi] * aux[:, 5 + lag : 6 + lag]
            total = total + ahead * taps_ref[lag : lag + 1, lo:hi]
            shifted = window_ref[8 - lag : 8 - lag + count, lo:hi] * aux[:, lag - 1 : lag]
            dtaps_ref[8 * lag : 8 * lag + 8, lo:hi] += jnp.sum(
                (here * shifted).reshape(count // 8, 8, block), axis=0
            )
        dproj_ref[:, lo:hi] = total.astype(jnp.bfloat16)
    later_ref[count : count + 8, :] = later_ref[0:8, :]
    later_out_ref[...] = later_ref[0:8, :]


FORWARD_CHUNKS = 4
BACKWARD_CHUNKS = 1


def whole_block(array):
    return pl.BlockSpec(array.shape, lambda step, rank: (0,) * array.ndim)


def turned_place(blocks, ranks):
    return lambda place, rank: lax.rem(place - rank[0] * (blocks // ranks) + blocks, blocks)


def mixer_forward(rank, proj, aux, segment_rows, taps, head_rows, gain, heads, dk, dv, ranks):
    length, width = proj.shape
    chunks = FORWARD_CHUNKS
    count = chunks * CHUNK
    steps = length // count
    conv_cols = heads * (2 * dk + dv)
    turned = turned_place(steps, ranks)
    rows = lambda cols: pl.BlockSpec((count, cols), lambda step, rank: (step, 0))
    turned_rows = lambda cols: pl.BlockSpec(
        (count, cols), lambda step, rank: (turned(step, rank), 0)
    )
    return pl.pallas_call(
        partial(forward_body, (heads, dk, dv, chunks)),
        grid_spec=pltpu.PrefetchScalarGridSpec(
            num_scalar_prefetch=1,
            grid=(steps,),
            in_specs=[
                turned_rows(width),
                rows(LANES),
                pl.BlockSpec((chunks, 1, CHUNK), lambda step, rank: (step, 0, 0)),
                whole_block(taps),
                whole_block(head_rows),
                whole_block(gain),
            ],
            out_specs=[
                turned_rows(heads * dv),
                rows(heads * dv),
                rows(heads * dv),
                pl.BlockSpec((chunks, dk, heads * dv), lambda step, rank: (step, 0, 0)),
                rows(heads * CHUNK),
            ],
            scratch_shapes=[
                pltpu.VMEM((8 + count, conv_cols), jnp.float32),
                pltpu.VMEM((heads, dk, dv), jnp.float32),
            ],
        ),
        out_shape=[
            jax.ShapeDtypeStruct((length, heads * dv), jnp.bfloat16),
            jax.ShapeDtypeStruct((length, heads * dv), jnp.float32),
            jax.ShapeDtypeStruct((length, heads * dv), jnp.float32),
            jax.ShapeDtypeStruct((length // CHUNK, dk, heads * dv), jnp.float32),
            jax.ShapeDtypeStruct((length, heads * CHUNK), jnp.float32),
        ],
        compiler_params=pltpu.CompilerParams(vmem_limit_bytes=48 * 2**20),
        cost_estimate=pl.CostEstimate(
            flops=80 * 10**9, bytes_accessed=length * width * 12, transcendentals=0
        ),
        name="mixer_forward",
    )(rank, proj, aux, segment_rows, taps, head_rows, gain)


def mixer_backward(
    rank,
    proj,
    aux,
    segment_rows,
    taps,
    head_rows,
    gain,
    saved,
    grad,
    heads,
    dk,
    dv,
    ranks,
    high,
    low,
    later,
    carried,
    dproj,
):
    held = [] if dproj is None else [dproj]
    length, width = proj.shape
    chunks = BACKWARD_CHUNKS
    count = chunks * CHUNK
    steps = length // count
    conv_cols = heads * (2 * dk + dv)
    out, fresh, states, inverses = saved
    place = lambda step: high - step
    turned = turned_place(steps, ranks)
    rows = lambda cols: pl.BlockSpec((count, cols), lambda step, rank: (place(step), 0))
    turned_rows = lambda cols: pl.BlockSpec(
        (count, cols), lambda step, rank: (turned(place(step), rank), 0)
    )
    lags = taps.shape[0]
    turned_eights = turned_place(length // 8, ranks)
    before = pl.BlockSpec(
        (8, width),
        lambda step, rank: (
            turned_eights(jnp.maximum(place(step) * (count // 8) - 1, 0), rank),
            0,
        ),
    )
    whole = lambda shape: pl.BlockSpec(shape, lambda step, rank: (0, 0))
    return pl.pallas_call(
        partial(backward_body, (heads, dk, dv, chunks, high), len(held)),
        grid_spec=pltpu.PrefetchScalarGridSpec(
            num_scalar_prefetch=1,
            grid=(high - low + 1,),
            in_specs=[
                turned_rows(width),
                before,
                rows(LANES),
                pl.BlockSpec((chunks, 1, CHUNK), lambda step, rank: (place(step), 0, 0)),
                whole_block(taps),
                whole_block(head_rows),
                whole_block(gain),
                rows(heads * dv),
                rows(heads * dv),
                pl.BlockSpec((chunks, dk, heads * dv), lambda step, rank: (place(step), 0, 0)),
                rows(heads * CHUNK),
                turned_rows(heads * dv),
                whole_block(later),
                whole_block(carried),
            ]
            + [pl.BlockSpec(memory_space=pl.ANY)] * len(held),
            out_specs=[
                turned_rows(width),
                whole((8 * lags, conv_cols)),
                whole((8, dv)),
                whole((16, LANES)),
                whole(later.shape),
                pl.BlockSpec(carried.shape, lambda step, rank: (0, 0, 0)),
            ],
            scratch_shapes=[
                pltpu.VMEM((8 + count, conv_cols), jnp.float32),
                pltpu.VMEM((8 + count, conv_cols), jnp.float32),
            ],
        ),
        out_shape=[
            jax.ShapeDtypeStruct((length, width), jnp.bfloat16),
            jax.ShapeDtypeStruct((8 * lags, conv_cols), jnp.float32),
            jax.ShapeDtypeStruct((8, dv), jnp.float32),
            jax.ShapeDtypeStruct((16, LANES), jnp.float32),
            jax.ShapeDtypeStruct(later.shape, jnp.float32),
            jax.ShapeDtypeStruct(carried.shape, jnp.float32),
        ],
        input_output_aliases={15: 0} if held else {},
        compiler_params=pltpu.CompilerParams(vmem_limit_bytes=48 * 2**20),
        cost_estimate=pl.CostEstimate(
            flops=160 * 10**9, bytes_accessed=length * width * 16, transcendentals=0
        ),
        name="mixer_backward",
    )(
        rank, proj, proj, aux, segment_rows, taps, head_rows, gain,
        out, fresh, states, inverses, grad, later, carried, *held,
    )


def segment_columns(segments):
    length = segments.shape[0]
    blocks = segments.reshape(-1, CHUNK)

    def earlier(lag):
        return jnp.concatenate([jnp.full((lag,), -1, jnp.int32), segments[:-lag]])

    def later(lag):
        return jnp.concatenate([segments[lag:], jnp.full((lag,), -1, jnp.int32)])

    same = [segments == earlier(lag) for lag in (1, 2, 3)]
    before = earlier(1).reshape(-1, CHUNK)[:, :1]
    same.append((blocks == before).reshape(length))
    same.append((blocks == blocks[:, -1:]).reshape(length))
    columns = [one.astype(jnp.float32) for one in same] + [segments.astype(jnp.float32)]
    columns += [(segments == later(lag)).astype(jnp.float32) for lag in (1, 2, 3)]
    table = jnp.stack(columns, axis=1)
    return jnp.pad(table, ((0, 0), (0, LANES - len(columns))))


UNIT_TILE = 256


def ffn_body(
    sizes,
    rows_ref,
    cot_ref,
    gated_ref,
    gain_ref,
    *refs,
):
    ranks, tiles, spans = sizes
    weight_refs = [refs[at * 4 : at * 4 + 4] for at in range(len(spans))]
    refs = refs[4 * len(spans) :]
    output_ref, dmiddle_ref, dgated_ref, dgain_ref = refs[:4]
    grads_refs = refs[4:6]
    ffn_steps(
        ranks,
        tiles,
        spans,
        rows_ref,
        cot_ref,
        gated_ref,
        gain_ref,
        weight_refs,
        output_ref,
        dmiddle_ref,
        dgated_ref,
        dgain_ref,
        grads_refs,
        *refs[6:],
    )


def ffn_steps(
    ranks,
    tiles,
    spans,
    rows_ref,
    cot_ref,
    gated_ref,
    gain_ref,
    weight_refs,
    output_ref,
    dmiddle_ref,
    dgated_ref,
    dgain_ref,
    grads_refs,
    middle_ref,
    total_ref,
    dsecond_ref,
    second_ref,
    second_turned_ref,
    cot_turned_ref,
    dattn_ref,
    dattn_turned_ref,
):
    step = pl.program_id(0)
    tokens, width = rows_ref.shape
    begin, end = ranks, ranks + ranks * tiles
    slabs = [slice(at, at + CHUNK) for at in range(0, tokens, CHUNK)]

    def flat(ref):
        return ref[...].reshape(width, ref.shape[-1])

    @pl.when(step == 0)
    def start():
        middle_ref[...] = rows_ref[...].astype(jnp.float32)

    def attend(w_out_ref):
        middle_ref[...] += contract(gated_ref[...], flat(w_out_ref), (1, 1))

    for (low, high), held in zip(spans, weight_refs):
        pl.when(jnp.logical_and(step >= low, step < high))(partial(attend, held[0]))

    @pl.when(step == begin)
    def second_norm():
        for slab in slabs:
            middle = middle_ref[slab, :]
            scale = lax.rsqrt(jnp.mean(middle * middle, axis=1, keepdims=True) + TINY)
            second = middle * scale * gain_ref[...]
            second_ref[slab, :] = second.astype(jnp.bfloat16)
            second_turned_ref[:, slab] = jnp.transpose(second).astype(jnp.bfloat16)
            cot_turned_ref[:, slab] = jnp.transpose(
                cot_ref[slab, :].astype(jnp.float32)
            ).astype(jnp.bfloat16)
        total_ref[...] = jnp.zeros(total_ref.shape, jnp.float32)
        dsecond_ref[...] = jnp.zeros(dsecond_ref.shape, jnp.float32)

    def units(w_gate_ref, w_up_ref, w_down_ref, grads_ref):
        w_gate, w_up, w_down = flat(w_gate_ref), flat(w_up_ref), flat(w_down_ref)
        second = second_ref[...]
        gate = contract(second, w_gate, (1, 0))
        up = contract(second, w_up, (1, 0))
        dhidden = contract(cot_ref[...], w_down, (1, 0))
        sig = sigmoid(gate)
        active = gate * sig
        hidden = (active * up).astype(jnp.bfloat16)
        dgate = (dhidden * up * (sig * (1.0 + gate * (1.0 - sig)))).astype(jnp.bfloat16)
        dup = (dhidden * active).astype(jnp.bfloat16)
        total_ref[...] += contract(hidden, w_down, (1, 1))
        dsecond_ref[...] += contract(dgate, w_gate, (1, 1)) + contract(dup, w_up, (1, 1))
        turned = second_turned_ref[...]
        tile = gate.shape[1]
        grads_ref[:, :tile] = contract(turned, dgate, (1, 0)).astype(jnp.bfloat16)
        grads_ref[:, tile : 2 * tile] = contract(turned, dup, (1, 0)).astype(jnp.bfloat16)
        grads_ref[:, 2 * tile :] = contract(cot_turned_ref[...], hidden, (1, 0)).astype(
            jnp.bfloat16
        )

    for (low, high), held in zip(spans, weight_refs):
        grads_ref = grads_refs[0 if low >= 2 else 1]
        pl.when(jnp.logical_and(step >= begin + low * tiles, step < begin + high * tiles))(
            partial(units, *held[1:], grads_ref)
        )

    @pl.when(step == end)
    def second_norm_back():
        dgain_ref[...] = jnp.zeros(dgain_ref.shape, jnp.float32)
        for slab in slabs:
            middle = middle_ref[slab, :]
            output_ref[slab, :] = (middle + total_ref[slab, :]).astype(jnp.bfloat16)
            scale = lax.rsqrt(jnp.mean(middle * middle, axis=1, keepdims=True) + TINY)
            normed = middle * scale
            dsecond = dsecond_ref[slab, :]
            dgain_ref[...] += jnp.sum((dsecond * normed).reshape(CHUNK // 8, 8, width), axis=0)
            scaled = dsecond * gain_ref[...]
            dmiddle = cot_ref[slab, :].astype(jnp.float32) + scale * (
                scaled - normed * jnp.mean(scaled * normed, axis=1, keepdims=True)
            )
            dmiddle_ref[slab, :] = dmiddle
            dattn_ref[slab, :] = dmiddle.astype(jnp.bfloat16)
            dattn_turned_ref[:, slab] = jnp.transpose(dmiddle).astype(jnp.bfloat16)

    def attend_back(w_out_ref):
        dgated_ref[...] = contract(dattn_ref[...], flat(w_out_ref), (1, 0)).astype(
            dgated_ref.dtype
        )
        cols = gated_ref.shape[1]
        last_ref = grads_refs[-1]
        last_ref[:, :cols] = contract(dattn_turned_ref[...], gated_ref[...], (1, 0)).astype(
            jnp.bfloat16
        )
        last_ref[:, cols:] = jnp.zeros((last_ref.shape[0], last_ref.shape[1] - cols), jnp.bfloat16)

    for (low, high), held in zip(spans, weight_refs):
        pl.when(jnp.logical_and(step >= end + low, step < end + high))(
            partial(attend_back, held[0])
        )


def ffn_block(rows, cot, gated, weights, spans, gain, value_cols, unit_cols):
    tokens, width = rows.shape
    ranks = spans[-1][1]
    grad_spans = [(2, ranks), (0, 2)]
    tiles = unit_cols // UNIT_TILE
    begin, end = ranks, ranks + ranks * tiles
    group = 3 * UNIT_TILE

    def edge(step):
        return jnp.where(step < end, jnp.minimum(step, ranks - 1), step - end)

    def out_spec(array, low, high):
        return pl.BlockSpec(
            (array.shape[0], 1, array.shape[2], value_cols),
            lambda step: (0, jnp.clip(edge(step) - low, 0, high - low - 1), 0, 0),
        )

    def tile_at(step, low, high):
        return jnp.clip(step - begin - low * tiles, 0, (high - low) * tiles - 1)

    def unit_spec(array, low, high, kind):
        first = value_cols // UNIT_TILE + kind * tiles

        def place(step):
            tile = tile_at(step, low, high)
            return (0, tile // tiles, 0, first + lax.rem(tile, tiles))

        return pl.BlockSpec((array.shape[0], 1, array.shape[2], UNIT_TILE), place)

    def grads_at(step, low, high):
        place = tile_at(step, low, high)
        return jnp.where(step < end, place, place + 1 + step - end) if low == 0 else place

    whole = lambda shape: pl.BlockSpec(shape, lambda step: (0,) * len(shape))
    bf, f32 = jnp.bfloat16, jnp.float32
    weight_specs, weight_args = [], []
    for array, (low, high) in zip(weights, spans):
        weight_specs.append(out_spec(array, low, high))
        weight_specs += [unit_spec(array, low, high, kind) for kind in range(3)]
        weight_args += [array] * 4
    late = lambda step: (0, jnp.maximum(step - end, 0))
    return pl.pallas_call(
        partial(ffn_body, (ranks, tiles, tuple(spans))),
        grid=(end + ranks,),
        in_specs=[
            whole(rows.shape),
            whole(cot.shape),
            pl.BlockSpec((tokens, value_cols), lambda step: (0, edge(step))),
            whole(gain.shape),
            *weight_specs,
        ],
        out_specs=[
            whole(rows.shape),
            whole(rows.shape),
            pl.BlockSpec((tokens, value_cols), late),
            whole((8, width)),
        ]
        + [
            pl.BlockSpec(
                (width, group), lambda step, low=low, high=high: (0, grads_at(step, low, high))
            )
            for low, high in grad_spans
        ],
        scratch_shapes=[
            pltpu.VMEM((tokens, width), f32),
            pltpu.VMEM((tokens, width), f32),
            pltpu.VMEM((tokens, width), f32),
            pltpu.VMEM((tokens, width), bf),
            pltpu.VMEM((width, tokens), bf),
            pltpu.VMEM((width, tokens), bf),
            pltpu.VMEM((tokens, width), bf),
            pltpu.VMEM((width, tokens), bf),
        ],
        out_shape=[
            jax.ShapeDtypeStruct(rows.shape, bf),
            jax.ShapeDtypeStruct(rows.shape, f32),
            jax.ShapeDtypeStruct((tokens, ranks * value_cols), bf),
            jax.ShapeDtypeStruct((8, width), f32),
        ]
        + [
            jax.ShapeDtypeStruct(
                (width, ((high - low) * tiles + (ranks if low == 0 else 0)) * group), bf
            )
            for low, high in grad_spans
        ],
        compiler_params=pltpu.CompilerParams(vmem_limit_bytes=60 * 2**20),
        cost_estimate=pl.CostEstimate(
            flops=35 * 10**9, bytes_accessed=60 * 10**6, transcendentals=0
        ),
        name="ffn_block",
    )(rows, cot, gated, gain, *weight_args)


def rms_back(grad, gain, normed, scale):
    scaled = grad * gain
    return scale * (scaled - normed * jnp.mean(scaled * normed, axis=-1, keepdims=True))


def padded(array, width):
    return jnp.pad(array, ((0, 0), (0, width - array.shape[1])))


def product(left, right, left_dim, right_dim):
    return lax.dot_general(
        left, right, (((left_dim,), (right_dim,)), ((), ())), preferred_element_type=jnp.float32
    )


def up_to(size, unit):
    return -(-size // unit) * unit


def fetched(block, ahead, ranks):
    return lax.ppermute(block, "tensor", [((i + ahead) % ranks, i) for i in range(ranks)])


def exchanged(blocks):
    ranks = len(blocks)
    result = [blocks[0]] + [None] * (ranks - 1)
    for ahead in range(1, ranks):
        if blocks[ahead] is None:
            continue
        result[ranks - ahead] = lax.ppermute(
            blocks[ahead], "tensor", [(i, (i + ahead) % ranks) for i in range(ranks)]
        )
    return result


def nothing_body(*refs):
    pass


def after(value, *earlier):
    return pl.pallas_call(
        nothing_body,
        in_specs=[pl.BlockSpec(memory_space=pl.ANY)] * (1 + len(earlier)),
        out_specs=pl.BlockSpec(memory_space=pl.ANY),
        out_shape=jax.ShapeDtypeStruct(value.shape, value.dtype),
        input_output_aliases={0: 0},
        name="after",
    )(value, *earlier)


def stacked_body(*refs):
    for at, ref in enumerate(refs[1:-1]):
        refs[-1][at] = ref[...]


def stacked_after(blocks, earlier):
    return pl.pallas_call(
        stacked_body,
        in_specs=[pl.BlockSpec(memory_space=pl.ANY)]
        + [pl.BlockSpec(memory_space=pltpu.VMEM)] * len(blocks),
        out_specs=pl.BlockSpec(memory_space=pltpu.VMEM),
        out_shape=jax.ShapeDtypeStruct((len(blocks), *blocks[0].shape), blocks[0].dtype),
        name="stacked_after",
    )(earlier, *blocks)


def summed_over(vector, axis):
    size = lax.axis_size(axis)
    apart = 1
    while apart < size:
        vector = vector + lax.ppermute(vector, axis, [(i, i ^ apart) for i in range(size)])
        apart *= 2
    return vector


def shards(
    layer_input,
    segments,
    norm_gain,
    w_query,
    w_key,
    w_value,
    w_outgate,
    w_beta,
    w_decay,
    conv_query,
    conv_key,
    conv_value,
    decay_log,
    decay_bias,
    out_gain,
    w_out,
    ffn_gain,
    w_gate,
    w_up,
    w_down,
    cotangent,
):
    tensor_rank = lax.axis_index("tensor")
    ranks = lax.axis_size("tensor")
    key_cols, value_cols, heads = w_query.shape[1], w_value.shape[1], w_beta.shape[1]
    dk, dv = key_cols // heads, value_cols // heads
    units = w_gate.shape[1]
    unit_cols = up_to(units, UNIT_TILE)
    tokens = layer_input.shape[0]
    conv_cols = 2 * key_cols + value_cols
    gate_at, small_at = conv_cols, conv_cols + value_cols

    joined = lax.all_gather(
        padded(
            jnp.concatenate([w_query, w_key, w_value, w_outgate, w_beta, w_decay], axis=1),
            small_at + LANES,
        ),
        "dp",
        axis=0,
        tiled=True,
    )
    rest_shard = jnp.concatenate(
        [w_out.T, padded(w_gate, unit_cols), padded(w_up, unit_cols), padded(w_down.T, unit_cols)],
        axis=1,
    )
    rest_shard = with_layout_constraint(rest_shard, Layout(major_to_minor=(0, 1)))

    near_rest = lax.all_gather(rest_shard[None], "dp")

    residual = layer_input.astype(jnp.float32)
    first_scale = lax.rsqrt(jnp.mean(residual * residual, axis=-1, keepdims=True) + TINY)
    first_normed = residual * first_scale
    first = (first_normed * norm_gain).astype(jnp.bfloat16)
    mixer_blocks = [first] + [fetched(first, ahead, ranks) for ahead in range(1, ranks)]
    mixer_rows = jnp.concatenate(mixer_blocks, axis=0)
    projected = product(mixer_rows, joined, 1, 0)

    rest_shard, _ = lax.optimization_barrier((rest_shard, mixer_blocks))
    far = [fetched(rest_shard, ahead, ranks) for ahead in range(1, ranks)]

    def local(array, width):
        return lax.dynamic_slice_in_dim(array, tensor_rank * width, width, array.ndim - 1)

    taps = jnp.concatenate(
        [local(conv_query, key_cols), local(conv_key, key_cols), local(conv_value, value_cols)],
        axis=1,
    )
    head_rows = jnp.pad(
        jnp.stack([local(decay_log, heads), local(decay_bias, heads)]),
        ((0, 6), (heads, LANES - 2 * heads)),
    )
    gain_row = out_gain[None, :]
    aux = segment_columns(segments)
    segment_rows = segments.astype(jnp.float32).reshape(-1, 1, CHUNK)
    rank = tensor_rank.astype(jnp.int32).reshape(1)
    ahead, projected = lax.optimization_barrier((far[0], projected))
    next_rest = lax.all_gather(ahead[None], "dp")
    gated, *saved = mixer_forward(
        rank, projected, aux, segment_rows, taps, head_rows, gain_row, heads, dk, dv, ranks
    )

    def token_blocks(array):
        return [array[at * tokens : (at + 1) * tokens] for at in range(ranks)]

    far_rest = lax.all_gather(stacked_after(far[1:], gated), "dp")
    gated_rows = jnp.concatenate(exchanged(token_blocks(gated)), axis=1)
    spans = [(0, 1), (1, 2), (2, ranks)]
    layer_output, grad_middle, grad_gated, dffn, far_grads, near_grads = ffn_block(
        layer_input,
        cotangent,
        gated_rows,
        [near_rest, next_rest, far_rest],
        spans,
        ffn_gain[None, :],
        value_cols,
        unit_cols,
    )

    def scattered(array):
        return lax.psum_scatter(array, "dp", scatter_dimension=0, tiled=True)

    summed_far = scattered(far_grads)
    span_cols = unit_cols // UNIT_TILE * 3 * UNIT_TILE
    received_far = exchanged(
        [None, None]
        + [summed_far[:, at * span_cols : (at + 1) * span_cols] for at in range(ranks - 2)]
    )
    grad_gated_rows = jnp.concatenate(
        exchanged(
            [grad_gated[:, at * value_cols : (at + 1) * value_cols] for at in range(ranks)]
        ),
        axis=0,
    )
    blocks = segments.shape[0] // (BACKWARD_CHUNKS * CHUNK)
    cut = blocks * 3 // 8
    later = jnp.zeros((8, conv_cols), jnp.float32)
    carried = jnp.zeros((heads, dk, dv), jnp.float32)
    grad_proj = None
    small_grads = []
    for high, low in ((blocks - 1, cut), (cut - 1, 0)):
        if low == 0:
            summed_near = scattered(after(near_grads, summed_far, later))
            later = after(later, summed_far)
        grad_proj, dtaps, dgain, dhead, later, carried = mixer_backward(
            rank,
            projected,
            aux,
            segment_rows,
            taps,
            head_rows,
            gain_row,
            saved,
            grad_gated_rows,
            heads,
            dk,
            dv,
            ranks,
            high,
            low,
            later,
            carried,
            grad_proj,
        )
        small_grads.append((dtaps, dgain, dhead))
    dtaps, dgain, dhead = (sum(parts) for parts in zip(*small_grads))
    back_first = [
        product(block, joined, 1, 1).astype(jnp.bfloat16) for block in token_blocks(grad_proj)
    ]
    grad_proj, _ = lax.optimization_barrier((grad_proj, back_first))
    grad_joined = product(mixer_rows, grad_proj, 0, 0)
    received_first = exchanged(back_first)
    grad_norm_gain = jnp.sum(joined.astype(jnp.float32) * grad_joined, axis=1) / norm_gain

    group = 3 * UNIT_TILE
    tiles = unit_cols // UNIT_TILE
    grad_joined_low = grad_joined.astype(jnp.bfloat16)
    summed_joined = scattered(grad_joined_low).astype(jnp.float32)
    out_at = 2 * span_cols
    near_sends = [
        summed_near[:, out_at : out_at + value_cols],
        jnp.concatenate(
            [
                summed_near[:, span_cols:out_at],
                summed_near[:, out_at + group : out_at + group + value_cols],
            ],
            axis=1,
        ),
    ] + [
        summed_near[:, out_at + at * group : out_at + at * group + value_cols]
        for at in range(2, ranks)
    ]

    lags = taps.shape[0]
    mine = jnp.concatenate(
        [
            jnp.sum(dtaps.reshape(lags, 8, conv_cols), axis=1).reshape(-1),
            jnp.sum(dhead[0:8], axis=0)[heads : 2 * heads],
            jnp.sum(dhead[8:16], axis=0)[heads : 2 * heads],
        ]
    )
    placed = jnp.where((jnp.arange(ranks) == tensor_rank)[:, None], mine[None, :], 0.0)
    vector = jnp.concatenate(
        [grad_norm_gain, jnp.sum(dffn, axis=0), jnp.sum(dgain, axis=0), placed.reshape(-1)]
    )
    vector = after(vector, *received_first[1:])
    vector = summed_over(vector, "dp")
    small = vector + sum(fetched(vector, ahead, ranks) for ahead in range(1, ranks))
    received_near = exchanged(near_sends)
    owned = sum(
        part.astype(jnp.float32)
        for part in [summed_near[:, :span_cols], received_near[ranks - 1][:, :span_cols]]
        + [part for part in received_far if part is not None]
    )
    owned_out = sum(
        part.astype(jnp.float32)
        for part in received_near[: ranks - 1] + [received_near[ranks - 1][:, span_cols:]]
    )
    by_kind = [
        jnp.concatenate(
            [
                owned[:, tile * group + kind * UNIT_TILE : tile * group + (kind + 1) * UNIT_TILE]
                for tile in range(tiles)
            ],
            axis=1,
        )[:, :units]
        for kind in range(3)
    ]
    received_first[1] = after(received_first[1], grad_joined_low)
    grad_first = sum(part.astype(jnp.float32) for part in received_first)
    grad_input = grad_middle + rms_back(grad_first, norm_gain, first_normed, first_scale)
    width = norm_gain.shape[0]
    sections = small[2 * width + dv :].reshape(ranks, -1)
    taps_all = sections[:, : lags * conv_cols].reshape(ranks, lags, conv_cols).transpose(1, 0, 2)
    logs_all = sections[:, lags * conv_cols :]

    def columns(lo, hi):
        return summed_joined[:, lo:hi]

    return (
        layer_output,
        grad_input,
        small[:width],
        columns(0, key_cols),
        columns(key_cols, 2 * key_cols),
        columns(2 * key_cols, conv_cols),
        columns(gate_at, small_at),
        columns(small_at, small_at + heads),
        columns(small_at + heads, small_at + 2 * heads),
        taps_all[:, :, :key_cols].reshape(lags, -1),
        taps_all[:, :, key_cols : 2 * key_cols].reshape(lags, -1),
        taps_all[:, :, 2 * key_cols :].reshape(lags, -1),
        logs_all[:, :heads].reshape(-1),
        logs_all[:, heads:].reshape(-1),
        small[2 * width : 2 * width + dv],
        owned_out.T,
        small[width : 2 * width],
        by_kind[0],
        by_kind[1],
        by_kind[2].T,
    )


def solution(mesh):
    in_specs = (
        P(("dp", "tensor"), None),
        P("dp"),
        P(),
        P("dp", "tensor"),
        P("dp", "tensor"),
        P("dp", "tensor"),
        P("dp", "tensor"),
        P("dp", "tensor"),
        P("dp", "tensor"),
        P(),
        P(),
        P(),
        P(),
        P(),
        P(),
        P("tensor", "dp"),
        P(),
        P("dp", "tensor"),
        P("dp", "tensor"),
        P("tensor", "dp"),
        P(("dp", "tensor"), None),
    )
    out_specs = (
        P(("dp", "tensor"), None),
        P(("dp", "tensor"), None),
        P(),
        P("dp", "tensor"),
        P("dp", "tensor"),
        P("dp", "tensor"),
        P("dp", "tensor"),
        P("dp", "tensor"),
        P("dp", "tensor"),
        P(),
        P(),
        P(),
        P(),
        P(),
        P(),
        P("tensor", "dp"),
        P(),
        P("dp", "tensor"),
        P("dp", "tensor"),
        P("tensor", "dp"),
    )
    return jax.shard_map(shards, mesh=mesh, in_specs=in_specs, out_specs=out_specs, check_vma=False)
```
